512 devices in a mesh: lon: 64 (over x_hi, z, core), lat: 8 (over x_lo, y).
Axes of the slice: x: 4 (x_hi: 2, x_lo: 2; x = x_hi * 2 + x_lo), y: 4, z: 16, core: 2. Of those that a mesh axis runs over, the one named last changes fastest.
Arguments:
- tokens: bfloat16 [2, 48, 768, 512], P(None, 'lat', 'lon'), may hold values from -16 to 16
- key_valid: int32 [2, 48, 768], P(None, 'lat', 'lon'), may hold values 0 or 1
- norm_gain: float32 [512], replicated, may hold values from 0.5 to 1.5
- w_qkv: bfloat16 [512, 1536], replicated, may hold values from -0.25 to 0.25
- bias_table: float32 [8, 759], replicated, may hold values from -4 to 4
- w_proj: bfloat16 [512, 512], replicated, may hold values from -0.25 to 0.25
- grad_out: bfloat16 [2, 48, 768, 512], P(None, 'lat', 'lon'), may hold values from -6 to 6
Outputs:
- result: bfloat16 [2, 48, 768, 512], P(None, 'lat', 'lon')
- grad_in: bfloat16 [2, 48, 768, 512], P(None, 'lat', 'lon')
- grad_qkv: float32 [512, 1536], P(('lon', 'lat'))
- grad_gain: float32 [512], replicated
- grad_bias: float32 [8, 759], replicated
The draws below stay inside these ranges and needn't reach their ends.
All inputs are finite; a program needn't handle non-finite values. No bound on the sum of `key_valid` on one device may be relied on, other than what follows from the above.
Results may differ from the reference program's by a relative error of at most 0.014.
Values may be sent and summed in bfloat16 or wider, within the bound.
A program may use at most 64 MiB of HBM per device.

```python
from functools import partial
import jax
import jax.numpy as jnp
from jax import lax

D = 512
HEADS = 8
LEVELS = 2
WLAT = 6
WLON = 12
NLAT = 48
NLON = 768
RELN = 759
N_LON = 64
N_LAT = 8


def set_ends(values, stream_key, smallest, top_value):
    dims = values.shape
    place = [jax.random.randint(jax.random.fold_in(stream_key, axis), (), 0, dims[axis]) for axis in range(len(dims))]
    values = values.at[tuple(place)].set(smallest)
    longest = dims.index(max(dims))
    place[longest] = (place[longest] + 1) % dims[longest]
    return values.at[tuple(place)].set(top_value)


def with_spikes(array, own_key, source, target, blocks, factor):
    def block_of(position):
        return (jnp.arange(array.shape[position]) // (array.shape[position] // blocks)).reshape((-1,) + (1,) * (array.ndim - 1 - position))

    first = jax.random.permutation(own_key, blocks)[block_of(target)]
    far = (block_of(target) + blocks // 2) % blocks
    return jnp.where((block_of(source) == first) | (block_of(source) == far), factor * array, array)


def shard_levels(own_key, extent, cuts, least, largest):
    factor_of, own = 1.0, jax.random.fold_in(own_key, 6)
    for axis_at, shards_of in cuts:
        steps = jnp.exp(jax.random.uniform(jax.random.fold_in(own, axis_at), (shards_of,), jnp.float32, least / len(cuts), largest / len(cuts)))
        factor_of = factor_of * jnp.repeat(steps, extent[axis_at] // shards_of).reshape([-1 if axis == axis_at else 1 for axis in range(len(extent))])
    return factor_of


def normal_values(own_key, extent, width, reach, split=(), kind=jnp.bfloat16):
    factor_of = shard_levels(own_key, extent, split, -0.22, 0.18) if split else 1.0
    values = jax.random.normal(own_key, extent, jnp.float32) * width * factor_of
    return jnp.minimum(jnp.maximum(values, -reach), reach).astype(kind)


def heavy_noise(own_key, shape, scale, limit, cuts, heavy, kind=jnp.bfloat16):
    array = scale * jax.random.normal(own_key, shape, jnp.float32)
    if cuts:
        array = array * shard_levels(own_key, shape, cuts, -0.22, 0.18)
    return jnp.clip(with_spikes(array, jax.random.fold_in(own_key, 3), *heavy), -limit, limit).astype(kind)


def setup_inputs(seed: int = 0) -> dict:
    seeds = jax.random.split(jax.random.key(seed), 8)
    return {
        "tokens": heavy_noise(seeds[0], (LEVELS, NLAT, NLON, D), 1.0, 16.0, ((1, 8), (2, 64)), (2, 3, 64, 4.0)),
        "key_valid": set_ends((jax.random.randint(seeds[1], (LEVELS, NLAT, NLON), 0, 8) < 7).astype(jnp.int32), jax.random.fold_in(seeds[1], 1), 0, 1),
        "norm_gain": jnp.clip(1.0 + 0.1 * jax.random.normal(seeds[2], (D,), jnp.float32), 0.5, 1.5),
        "w_qkv": normal_values(seeds[3], (D, 3 * D), D ** -0.5, 0.25),
        "bias_table": normal_values(seeds[4], (HEADS, RELN), 1.0, 4.0, (), jnp.float32),
        "w_proj": normal_values(seeds[5], (D, D), D ** -0.5, 0.25),
        "grad_out": normal_values(seeds[6], (LEVELS, NLAT, NLON, D), 1.0, 6.0, ((1, 8), (2, 64))),
    }


def layer_norm(values, norm_gain):
    centred = values - lax.optimization_barrier(jnp.mean(values, axis=-1, keepdims=True))
    spread = lax.optimization_barrier(jnp.mean(centred * centred, axis=-1, keepdims=True))
    return (centred * lax.rsqrt(spread + 1e-05) * norm_gain).astype(jnp.bfloat16)

def relative_index():
    window_size = LEVELS * WLAT * WLON
    places = jnp.arange(window_size, dtype=jnp.int32)
    level_pos = places // (WLAT * WLON)
    row_pos = places // WLON % WLAT
    col_pos = places % WLON
    level_gap = level_pos[:, None] - level_pos[None, :] + (LEVELS - 1)
    row_gap = row_pos[:, None] - row_pos[None, :] + (WLAT - 1)
    col_gap = col_pos[:, None] - col_pos[None, :] + (WLON - 1)
    return ((level_gap * (2 * WLAT - 1) + row_gap) * (2 * WLON - 1) + col_gap).astype(jnp.int32)

def allowance(region, key_mask):
    window_size = region.shape[1]
    same_region = (region[:, :, None] == region[:, None, :]).astype(jnp.float32)
    self_mask = jnp.eye(window_size, dtype=jnp.float32)
    return same_region * jnp.maximum(key_mask[:, None, :], self_mask[None])

def attend(qkv_act, bias_table, allowed, rel_index):
    window_count, window_size, triple = qkv_act.shape
    head_count = bias_table.shape[0]
    head_size = triple // (3 * head_count)
    pieces = qkv_act.reshape(window_count, window_size, 3, head_count, head_size)
    scores = jnp.einsum('wqhd,wkhd->whqk', pieces[:, :, 0].astype(jnp.float32), pieces[:, :, 1].astype(jnp.float32))
    scores = scores * head_size ** (-0.5) + jnp.take(bias_table, rel_index, axis=1)[None]
    weights = jnp.exp(scores) * allowed[:, None]
    attention = (weights / lax.optimization_barrier(jnp.sum(weights, axis=-1, keepdims=True))).astype(jnp.bfloat16)
    mixed = jnp.einsum('whqk,wkhd->wqhd', attention.astype(jnp.float32), pieces[:, :, 2].astype(jnp.float32))
    return mixed.astype(jnp.bfloat16).reshape(window_count * window_size, head_count * head_size)

def window_pass(windows, allowed, w_qkv, bias_table, w_proj, rel_index, cot_windows):
    window_count, window_size, feature_width = windows.shape
    flat_rows = windows.reshape(window_count * window_size, feature_width)
    qkv_act = jnp.dot(flat_rows, w_qkv, preferred_element_type=jnp.float32).astype(jnp.bfloat16)
    mixed, pullback = jax.vjp(partial(attend, allowed=allowed, rel_index=rel_index), qkv_act.reshape(window_count, window_size, -1), bias_table)
    attn_out = jnp.dot(mixed, w_proj, preferred_element_type=jnp.float32).astype(jnp.bfloat16)
    cot_rows = cot_windows.reshape(window_count * window_size, feature_width)
    grad_mixed = lax.dot_general(cot_rows, w_proj, (((1,), (1,)), ((), ())), preferred_element_type=jnp.float32).astype(jnp.bfloat16)
    grad_act, grad_table = pullback(grad_mixed)
    grad_act = grad_act.reshape(window_count * window_size, -1)
    grad_rows = lax.dot_general(grad_act, w_qkv, (((1,), (1,)), ((), ())), preferred_element_type=jnp.float32).astype(jnp.bfloat16)
    grad_weight = lax.dot_general(flat_rows, grad_act, (((0,), (0,)), ((), ())), preferred_element_type=jnp.float32)
    return (attn_out.reshape(windows.shape), grad_rows.reshape(windows.shape), grad_weight, grad_table)

def to_windows(grid):
    levels, row_count, col_count = grid.shape[:3]
    trailing = grid.shape[3:]
    split_grid = grid.reshape((levels, row_count // WLAT, WLAT, col_count // WLON, WLON) + trailing)
    axis_order = (3, 1, 0, 2, 4) + tuple(range(5, 5 + len(trailing)))
    return split_grid.transpose(axis_order).reshape((col_count // WLON, row_count // WLAT, levels * WLAT * WLON) + trailing)

def from_windows(blocks, levels):
    col_blocks, row_blocks = blocks.shape[:2]
    trailing = blocks.shape[3:]
    split_grid = blocks.reshape((col_blocks, row_blocks, levels, WLAT, WLON) + trailing)
    axis_order = (2, 1, 3, 0, 4) + tuple(range(5, 5 + len(trailing)))
    return split_grid.transpose(axis_order).reshape((levels, row_blocks * WLAT, col_blocks * WLON) + trailing)

def reference(tokens, key_valid, norm_gain, w_qkv, bias_table, w_proj, grad_out):
    half_lat = WLAT // 2
    half_lon = WLON // 2
    levels, row_count, col_count, feature_width = tokens.shape
    values = tokens.astype(jnp.float32)
    normed, norm_pullback = jax.vjp(layer_norm, values, norm_gain)
    shifted = jnp.roll(normed, (-half_lat, -half_lon), axis=(1, 2))
    key_shift = jnp.roll(key_valid, (-half_lat, -half_lon), axis=(1, 2)).astype(jnp.float32)
    cot_shift = jnp.roll(grad_out, (-half_lat, -half_lon), axis=(1, 2))
    row_anchor = (jnp.arange(row_count, dtype=jnp.int32) + half_lat) % row_count
    region = jnp.broadcast_to((row_anchor < half_lat).astype(jnp.int32)[None, :, None], (levels, row_count, col_count))
    rel_index = relative_index()

    def window_step(totals, window_item):
        windows, regions, key_mask, cot_windows = window_item
        allowed = allowance(regions, key_mask)
        attn_out, grad_rows, grad_weight, grad_table = window_pass(windows, allowed, w_qkv, bias_table, w_proj, rel_index, cot_windows)
        return ((totals[0] + grad_weight, totals[1] + grad_table), (attn_out, grad_rows))
    start_sums = (jnp.zeros((feature_width, w_qkv.shape[1]), jnp.float32), jnp.zeros(bias_table.shape, jnp.float32))
    sums, outputs = lax.scan(window_step, start_sums, (to_windows(shifted), to_windows(region), to_windows(key_shift), to_windows(cot_shift)))
    attention_grid = jnp.roll(from_windows(outputs[0], levels), (half_lat, half_lon), axis=(1, 2))
    result = (values + attention_grid.astype(jnp.float32)).astype(jnp.bfloat16)
    grad_normed = jnp.roll(from_windows(outputs[1], levels), (half_lat, half_lon), axis=(1, 2))
    grad_values, grad_gain = norm_pullback(grad_normed)
    grad_in = (grad_out.astype(jnp.float32) + grad_values).astype(jnp.bfloat16)
    grad_qkv = sums[0].reshape(N_LON * N_LAT, -1)
    return (result, grad_in, grad_qkv, grad_gain, sums[1])
```

```python
import jax
import jax.numpy as jnp
import numpy as np
from jax import lax
from jax.experimental import pallas as pl
from jax.experimental.pallas import tpu as pltpu
from jax.sharding import PartitionSpec as P

MESH = pl.DeviceIdType.MESH
F32 = jnp.float32
BF16 = jnp.bfloat16

LEVELS, WLAT, WLON = 2, 6, 12
WIN = LEVELS * WLAT * WLON
D = 512
HEADS = 8
PAIRS = HEADS // 2
RELN = 759
RELP = 768
N_LON, N_LAT = 64, 8
N_Z = 16
N_PLANE = 16
MSG = 80
CHUNK = 3 * 128


def offset_of(t):
    level, row, col = t // 72, t // 12 % 6, t % 12
    return 253 * level + 23 * row + col


def make_tables():
    pack = np.zeros((4 * MSG, 2 * 192), np.float32)
    unpack = np.zeros((304, 4 * MSG), np.float32)
    key_col = np.zeros((128, D), np.float32)
    key_row = np.zeros((4, 16, D), np.float32)
    for l in range(LEVELS):
        for r in range(WLAT):
            for c in range(WLON):
                quad = (r // 3) * 2 + c // 6
                place = l * 18 + (r % 3) * 6 + c % 6
                t = WIN - 1 - (l * 72 + ((r + 3) % 6) * 12 + (c + 6) % 12)
                for a in range(2):
                    msg = quad * MSG + a * 36 + place
                    pack[msg, a * 192 + (l * 6 + r) * 16 + c] = 1
                    unpack[a * WIN + t, msg] = 1
                key_col[c, t] = 1
                key_row[quad, l * 8 + r, t] = 1
    for quad in range(4):
        unpack[2 * WIN, quad * MSG + 72] = 1
    perm = np.zeros((D, D), np.float32)
    for core in range(2):
        for xh in range(2):
            for lat in range(8):
                for z in range(16):
                    perm[core * 256 + (xh * 8 + lat) * 16 + z, xh * 256 + z * 16 + core * 8 + lat] = 1
    pick = np.zeros((6, WIN, RELP), np.float32)
    for g in range(6):
        for k in range(WIN):
            pick[g, k, (379 + offset_of(k) - 253 * (g // 3) - 46 * (g % 3)) % RELP] = 1
    step = np.arange(24)
    step = np.tile(23 * (step // 12) + step % 12, HEADS)
    skew = np.broadcast_to(step[:, None], (192, 128)).astype(np.int32)
    t = np.arange(WIN)
    half = ((WIN - 1 - t) // 12 % 6) >= 3
    masks = np.stack([half[:, None] != half[None, :], np.eye(WIN, dtype=bool)]).astype(np.float32)
    as_bf16 = lambda v: jnp.asarray(v, BF16)
    return (
        as_bf16(pack),
        as_bf16(unpack),
        as_bf16(pack.T),
        as_bf16(unpack[: 2 * WIN].T),
        as_bf16(key_col),
        jnp.asarray(key_row),
        as_bf16(perm),
        as_bf16(pick),
        jnp.asarray(skew),
        jnp.asarray(masks),
    )


def dot(a, b):
    return lax.dot_general(a, b, (((1,), (0,)), ((), ())), preferred_element_type=F32)


def dot_nt(a, b):
    return lax.dot_general(a, b, (((1,), (1,)), ((), ())), preferred_element_type=F32)


def dot_tn(a, b):
    return lax.dot_general(a, b, (((0,), (0,)), ((), ())), preferred_element_type=F32)


def skewed(rows, skew, left):
    for bit in (1, 2, 4, 8, 16, 32):
        moved = pltpu.roll(rows, RELP - bit if left else bit, 1)
        rows = jnp.where((skew & bit) != 0, moved, rows)
    return rows


def kernel(
    tok, kv, gain, w_qkv, table, w_proj, gout,
    pack, unpack, pack_t, unpack_t, key_col, key_row, perm, pick, skew_ref, masks,
    result, grad_in, grad_qkv, grad_gain, grad_bias,
    flat, kvs, tabs, hsend, hrecv, bsend, brecv, bias, allowed, dscore,
    qkvs, gms, mixs, dqkv, s1, r1, s2, r2, s3, r3, ex, exr, exc, rx2, rx3, rx4,
    sem_hs, sem_hr, sem_bs, sem_br, sem_s1, sem_r1, sem_s2, sem_r2, sem_s3, sem_r3, sem_xs, sem_xr,
):
    lon, lat = lax.axis_index("lon"), lax.axis_index("lat")
    xh, zc = lax.div(lon, 32), lax.rem(lon, 32)
    z, core = lax.div(zc, 2), lax.rem(zc, 2)
    plane = xh * 8 + lat
    west, east = lax.rem(lon + N_LON - 1, N_LON), lax.rem(lon + 1, N_LON)
    north, south = lax.rem(lat + N_LAT - 1, N_LAT), lax.rem(lat + 1, N_LAT)
    twin = {"lon": lon + 1 - 2 * core, "lat": lat}
    halo_to = ({"lon": west, "lat": north}, {"lon": lon, "lat": north}, {"lon": west, "lat": lat})
    back_to = ({"lon": east, "lat": south}, {"lon": lon, "lat": south}, {"lon": east, "lat": lat})

    def plane_at(d):
        other = lax.rem(plane + d, N_PLANE)
        return other, {"lon": lax.div(other, 8) * 32 + zc, "lat": lax.rem(other, 8)}

    def z_at(d):
        other = lax.rem(z + d, N_Z)
        return other, {"lon": xh * 32 + other * 2 + core, "lat": lat}

    def send(src, dst, send_sem, recv_sem, to):
        pltpu.make_async_remote_copy(
            src_ref=src, dst_ref=dst, send_sem=send_sem, recv_sem=recv_sem,
            device_id=to, device_id_type=MESH,
        ).start()

    def wait(ref, sem):
        pltpu.make_async_copy(ref, ref, sem).wait()

    barrier = pltpu.get_barrier_semaphore()
    for to in halo_to + back_to + (twin,):
        pl.semaphore_signal(barrier, inc=1, device_id=to, device_id_type=MESH)

    def greet(d, carry):
        pl.semaphore_signal(barrier, inc=1, device_id=plane_at(d)[1], device_id_type=MESH)
        pl.semaphore_signal(barrier, inc=1, device_id=z_at(d)[1], device_id_type=MESH)
        return carry

    lax.fori_loop(1, 16, greet, 0)

    flat[...] = jnp.zeros_like(flat)
    for a, ref in enumerate((tok, gout)):
        for l in range(LEVELS):
            for r in range(WLAT):
                flat[a * 12 + l * 6 + r, 0:WLON, :] = ref[l, r]
    kvs[...] = jnp.zeros_like(kvs)
    for l in range(LEVELS):
        kvs[l * 8 : l * 8 + WLAT, 0:WLON] = kv[l].astype(F32)
    msg = dot(pack[...], flat[...].reshape(2 * 192, D))
    keys = dot(kvs[...].astype(BF16), key_col[...])
    row_at = lax.broadcasted_iota(jnp.int32, (MSG, D), 0)
    for quad in range(4):
        key_line = jnp.sum(keys * key_row[quad], axis=0, keepdims=True)
        block = jnp.where(row_at == 72, key_line, msg[quad * MSG : (quad + 1) * MSG]).astype(BF16)
        if quad == 3:
            hrecv[3] = block
        else:
            hsend[quad] = block

    pl.semaphore_wait(barrier, 37)
    for quad in range(3):
        send(hsend.at[quad], hrecv.at[quad], sem_hs.at[quad], sem_hr.at[quad], halo_to[quad])

    tabs[...] = jnp.zeros_like(tabs)
    tabs[:, 0:RELN] = table[...]
    skew = jnp.broadcast_to(skew_ref[:, 0:1], (192, RELP))
    rows = jnp.concatenate(
        [jnp.broadcast_to(tabs[h : h + 1, :], (24, RELP)) for h in range(HEADS)], axis=0
    )
    rows = skewed(rows, skew, False)
    high = rows.astype(BF16)
    low = (rows - high.astype(F32)).astype(BF16)
    both = jnp.concatenate([high, low], axis=0)
    for g in range(6):
        part = dot_nt(both, pick[g])
        part = part[:192] + part[192:]
        for h in range(HEADS):
            bias[h, g * 24 : (g + 1) * 24, :] = part[h * 24 : (h + 1) * 24]

    for quad in range(3):
        wait(hrecv.at[quad], sem_hr.at[quad])
    window = dot(unpack[...], hrecv[...].reshape(4 * MSG, D))
    x = window[0:WIN]
    cot = window[WIN : 2 * WIN]
    key_ok = window[2 * WIN : 2 * WIN + 1, 0:WIN]
    edge = (lat == N_LAT - 1).astype(F32)
    allowed[...] = (1.0 - edge * masks[0]) * jnp.maximum(key_ok, masks[1])

    centred = x - jnp.mean(x, axis=-1, keepdims=True)
    spread = jnp.mean(centred * centred, axis=-1, keepdims=True)
    rstd = lax.rsqrt(spread + 1e-5)
    xhat = centred * rstd
    normed = (xhat * gain[...]).astype(BF16)
    act = dot(normed, w_qkv[...]).astype(BF16)
    grad_mixed = dot_nt(cot.astype(BF16), w_proj[...]).astype(BF16)
    for j in range(12):
        qkvs[j] = act[:, j * 128 : (j + 1) * 128]
    for j in range(4):
        gms[j] = grad_mixed[:, j * 128 : (j + 1) * 128]
    normed_t = dot_nt(perm[...], normed).astype(BF16)
    first = lax.broadcasted_iota(jnp.int32, (WIN, 128), 1) < 64

    def plane_step(p):
        wait(r1.at[p], sem_r1.at[p])
        s2[p] = (s1[p, core].astype(F32) + r1[p].astype(F32)).astype(BF16).reshape(N_PLANE, N_Z, CHUNK)

        def one(d, carry):
            other, to = plane_at(d)
            send(s2.at[p, other], r2.at[p, d - 1], sem_s2.at[p], sem_r2.at[p], to)
            return carry

        lax.fori_loop(1, N_PLANE, one, 0)

    for p in range(PAIRS):
        q2, k2, v2, gm2 = qkvs[p], qkvs[4 + p], qkvs[8 + p], gms[p]
        zero = jnp.zeros_like(q2)
        mixed = dq = dk = dv = jnp.zeros((WIN, 128), F32)
        for s in range(2):
            h = 2 * p + s
            mine = first if s == 0 else jnp.logical_not(first)
            qm = jnp.where(mine, q2, zero) * jnp.asarray(0.125, BF16)
            km = jnp.where(mine, k2, zero)
            vm = jnp.where(mine, v2, zero)
            gm = jnp.where(mine, gm2, zero)
            weights = jnp.exp(dot_nt(qm, k2) + bias[h]) * allowed[...]
            probs = weights / jnp.sum(weights, axis=-1, keepdims=True)
            attention = probs.astype(BF16)
            mixed = mixed + dot(attention, vm)
            grad_att = dot_nt(gm, v2).astype(BF16).astype(F32)
            pull = probs * grad_att
            grad_scores = pull - probs * jnp.sum(pull, axis=-1, keepdims=True)
            dscore[h] = grad_scores
            short = grad_scores.astype(BF16)
            dq = dq + dot(short, km)
            dk = dk + dot_tn(short, qm)
            dv = dv + dot_tn(attention, gm)
        mixs[:, p * 128 : (p + 1) * 128] = mixed.astype(BF16)
        for j, part in enumerate((dq * 0.125, dk, dv)):
            dqkv[:, j * D + p * 128 : j * D + (p + 1) * 128] = part.astype(BF16)
        act_part = jnp.concatenate([(dq * 0.125).astype(BF16), dk.astype(BF16), dv.astype(BF16)], axis=1)
        s1[p] = dot(normed_t, act_part).astype(BF16).reshape(2, 256, CHUNK)
        send(s1.at[p, 1 - core], r1.at[p], sem_s1.at[p], sem_r1.at[p], twin)
        if p > 0:
            plane_step(p - 1)
    plane_step(PAIRS - 1)

    grad_normed = dot_nt(dqkv[...], w_qkv[...]).astype(BF16).astype(F32)
    grad_hat = grad_normed * gain[...]
    shift = jnp.mean(grad_hat, axis=-1, keepdims=True)
    slope = jnp.mean(grad_hat * xhat, axis=-1, keepdims=True)
    dx = (cot + rstd * (grad_hat - shift - xhat * slope)).astype(BF16)
    out = (x + dot(mixs[...], w_proj[...]).astype(BF16).astype(F32)).astype(BF16)
    back = dot(unpack_t[...], jnp.concatenate([out, dx], axis=0)).astype(BF16)
    for quad in range(3):
        bsend[quad] = back[quad * MSG : (quad + 1) * MSG]
        send(bsend.at[quad], brecv.at[quad], sem_bs.at[quad], sem_br.at[quad], back_to[quad])
    brecv[3] = back[3 * MSG :]

    gain_part = jnp.sum(grad_normed * xhat, axis=0, keepdims=True)
    ex[...] = jnp.zeros_like(ex)
    for j in range(4):
        ex[6, j : j + 1, :] = gain_part[:, j * 128 : (j + 1) * 128]
    table_rows = jnp.zeros((192, RELP), F32)
    for g in range(6):
        group = jnp.concatenate([dscore[h, g * 24 : (g + 1) * 24, :] for h in range(HEADS)], axis=0)
        table_rows = table_rows + dot(group.astype(BF16), pick[g])
    table_rows = skewed(table_rows, skew, True)
    table_part = jnp.sum(table_rows.reshape(HEADS, 24, RELP), axis=1)
    for j in range(6):
        ex[j] = table_part[:, j * 128 : (j + 1) * 128]
    send(ex.at[0:7], exr, sem_xs.at[0], sem_xr.at[0], twin)
    wait(exr, sem_xr.at[0])
    exc[...] = ex[...]
    exc[0:7] = ex[0:7] + exr[...]

    def share_plane(d, carry):
        other, to = plane_at(d)
        send(exc.at[other], rx2.at[d - 1], sem_xs.at[1], sem_xr.at[1], to)
        return carry

    lax.fori_loop(1, N_PLANE, share_plane, 0)
    wait(rx2, sem_xr.at[1])
    rx3[z] = exc[plane] + jnp.sum(rx2[...], axis=0)

    def share_z(d, carry):
        send(rx3.at[z], rx3.at[z], sem_xs.at[2], sem_xr.at[2], z_at(d)[1])
        return carry

    lax.fori_loop(1, N_Z, share_z, 0)

    for p in range(PAIRS):
        wait(r2.at[p], sem_r2.at[p])
        total = s2[p, plane].astype(F32)
        for d in range(N_PLANE - 1):
            total = total + r2[p, d].astype(F32)
        for row in range(N_Z):
            s3[row, :, p * CHUNK : (p + 1) * CHUNK] = total[row : row + 1]

    def spread_z(d, carry):
        other, to = z_at(d)
        send(s3.at[other], r3.at[d - 1], sem_s3, sem_r3, to)
        return carry

    lax.fori_loop(1, N_Z, spread_z, 0)

    wait(rx3.at[0:15], sem_xr.at[2])
    wait(rx3.at[0:15], sem_xs.at[2])
    rx4[plane] = jnp.sum(rx3[...], axis=0)

    def share_back(d, carry):
        send(rx4.at[plane], rx4.at[plane], sem_xs.at[3], sem_xr.at[3], plane_at(d)[1])
        return carry

    lax.fori_loop(1, N_PLANE, share_back, 0)

    for quad in range(3):
        wait(brecv.at[quad], sem_br.at[quad])
    done = dot(pack_t[...], brecv[...].reshape(4 * MSG, D)).astype(BF16)
    for a, ref in enumerate((result, grad_in)):
        for l in range(LEVELS):
            for r in range(WLAT):
                at = (a * 12 + l * 6 + r) * 16
                ref[l, r] = done[at : at + WLON]

    wait(r3, sem_r3)
    line = s3[z] + jnp.sum(r3[...], axis=0)
    for p in range(PAIRS):
        for j in range(3):
            grad_qkv[:, j * D + p * 128 : j * D + (p + 1) * 128] = line[:, p * CHUNK + j * 128 : p * CHUNK + (j + 1) * 128]

    wait(rx4.at[0:15], sem_xr.at[3])
    for j in range(4):
        grad_gain[:, j * 128 : (j + 1) * 128] = rx4[6, j : j + 1, :]
    for j in range(6):
        width = min(128, RELN - j * 128)
        grad_bias[:, j * 128 : j * 128 + width] = rx4[j, :, 0:width]

    for quad in range(3):
        wait(hsend.at[quad], sem_hs.at[quad])
        wait(bsend.at[quad], sem_bs.at[quad])
    for p in range(PAIRS):
        wait(r1.at[p], sem_s1.at[p])
        wait(r2.at[p], sem_s2.at[p])
    wait(r3, sem_s3)
    wait(exr, sem_xs.at[0])
    wait(rx2, sem_xs.at[1])
    wait(rx4.at[0:15], sem_xs.at[3])


def local(tokens, key_valid, norm_gain, w_qkv, bias_table, w_proj, grad_out):
    vmem = pl.BlockSpec(memory_space=pltpu.VMEM)
    tables = make_tables()
    dma = pltpu.SemaphoreType.DMA
    result, grad_in, grad_qkv, grad_gain, grad_bias = pl.pallas_call(
        kernel,
        out_shape=(
            jax.ShapeDtypeStruct(tokens.shape, BF16),
            jax.ShapeDtypeStruct(tokens.shape, BF16),
            jax.ShapeDtypeStruct((1, 3 * D), F32),
            jax.ShapeDtypeStruct((1, D), F32),
            jax.ShapeDtypeStruct((HEADS, RELN), F32),
        ),
        in_specs=[vmem] * (7 + len(tables)),
        out_specs=[vmem] * 5,
        scratch_shapes=[
            pltpu.VMEM((24, 16, D), BF16),
            pltpu.VMEM((16, 128), F32),
            pltpu.VMEM((HEADS, RELP), F32),
            pltpu.VMEM((3, MSG, D), BF16),
            pltpu.VMEM((4, MSG, D), BF16),
            pltpu.VMEM((3, MSG, D), BF16),
            pltpu.VMEM((4, MSG, D), BF16),
            pltpu.VMEM((HEADS, WIN, WIN), F32),
            pltpu.VMEM((WIN, WIN), F32),
            pltpu.VMEM((HEADS, WIN, WIN), F32),
            pltpu.VMEM((12, WIN, 128), BF16),
            pltpu.VMEM((4, WIN, 128), BF16),
            pltpu.VMEM((WIN, D), BF16),
            pltpu.VMEM((WIN, 3 * D), BF16),
            pltpu.VMEM((PAIRS, 2, 256, CHUNK), BF16),
            pltpu.VMEM((PAIRS, 256, CHUNK), BF16),
            pltpu.VMEM((PAIRS, N_PLANE, N_Z, CHUNK), BF16),
            pltpu.VMEM((PAIRS, N_PLANE - 1, N_Z, CHUNK), BF16),
            pltpu.VMEM((N_Z, 1, 3 * D), F32),
            pltpu.VMEM((N_Z - 1, 1, 3 * D), F32),
            pltpu.VMEM((16, 8, 128), F32),
            pltpu.VMEM((7, 8, 128), F32),
            pltpu.VMEM((16, 8, 128), F32),
            pltpu.VMEM((15, 8, 128), F32),
            pltpu.VMEM((16, 8, 128), F32),
            pltpu.VMEM((16, 8, 128), F32),
            dma((3,)), dma((3,)), dma((3,)), dma((3,)),
            dma((PAIRS,)), dma((PAIRS,)), dma((PAIRS,)), dma((PAIRS,)),
            dma, dma, dma((4,)), dma((4,)),
        ],
        compiler_params=pltpu.CompilerParams(
            collective_id=0, has_side_effects=True, vmem_limit_bytes=48 * 1024 * 1024
        ),
        name="window_block",
    )(tokens, key_valid, norm_gain.reshape(1, D), w_qkv, bias_table, w_proj, grad_out, *tables)
    return result, grad_in, grad_qkv, grad_gain.reshape(D), grad_bias


def solution(mesh):
    placed = (
        P(None, "lat", "lon", None),
        P(None, "lat", "lon"),
        P(),
        P(),
        P(),
        P(),
        P(None, "lat", "lon", None),
    )
    return jax.shard_map(
        local,
        mesh=mesh,
        in_specs=placed,
        out_specs=(
            P(None, "lat", "lon", None),
            P(None, "lat", "lon", None),
            P(("lon", "lat"), None),
            P(),
            P(),
        ),
        check_vma=False,
    )
```

```python
import jax
import jax.numpy as jnp
import numpy as np
from jax import lax
from jax.experimental import pallas as pl
from jax.experimental.pallas import tpu as pltpu
from jax.sharding import PartitionSpec as P

MESH = pl.DeviceIdType.MESH
F32 = jnp.float32
BF16 = jnp.bfloat16

LEVELS, WLAT, WLON = 2, 6, 12
WIN = LEVELS * WLAT * WLON
D = 512
HEADS = 8
PAIRS = HEADS // 2
RELN = 759
RELP = 768
N_LON, N_LAT = 64, 8
N_Z = 16
N_PLANE = 16
CHUNK = 3 * 128
VMEM_LIMIT = 60 * 1024 * 1024


def offset_of(t):
    level, row, col = t // 72, t // 12 % 6, t % 12
    return 253 * level + 23 * row + col


def make_tables():
    key_col = np.zeros((128, 256), np.float32)
    key_row = np.zeros((4, 16, 256), np.float32)
    for l in range(LEVELS):
        for r in range(WLAT):
            for c in range(WLON):
                t = l * 72 + ((r + 3) % 6) * 12 + (c + 6) % 12
                key_col[c, t] = 1
                key_row[(r // 3) * 2 + c // 6, r * 2 + l, t] = 1
    perm = np.zeros((D, D), np.float32)
    for core in range(2):
        for xh in range(2):
            for lat in range(8):
                for z in range(16):
                    perm[core * 256 + (xh * 8 + lat) * 16 + z, xh * 256 + z * 16 + core * 8 + lat] = 1
    pick = np.zeros((6, WIN, RELP), np.float32)
    for g in range(6):
        for k in range(WIN):
            pick[g, k, (379 + 253 * (g // 3) + 46 * (g % 3) - offset_of(k)) % RELP] = 1
    step = np.arange(24)
    step = np.tile(23 * (step // 12) + step % 12, HEADS)
    skew = np.broadcast_to(step[:, None], (192, 128)).astype(np.int32)
    half = np.arange(WIN) // 12 % 6 >= 3
    masks = np.stack([half[:, None] != half[None, :], np.eye(WIN, dtype=bool)]).astype(np.float32)
    as_bf16 = lambda v: jnp.asarray(v, BF16)
    return (
        as_bf16(key_col),
        jnp.asarray(key_row),
        jnp.asarray(skew),
        as_bf16(pick),
        jnp.asarray(masks),
        as_bf16(perm),
    )


def dot(a, b):
    return lax.dot_general(a, b, (((1,), (0,)), ((), ())), preferred_element_type=F32)


def dot_nt(a, b):
    return lax.dot_general(a, b, (((1,), (1,)), ((), ())), preferred_element_type=F32)


def dot_tn(a, b):
    return lax.dot_general(a, b, (((0,), (0,)), ((), ())), preferred_element_type=F32)


def skewed(rows, skew, left):
    for bit in (1, 2, 4, 8, 16, 32):
        moved = pltpu.roll(rows, RELP - bit if left else bit, 1)
        rows = jnp.where((skew & bit) != 0, moved, rows)
    return rows


def window_part(ref, quad):
    return ref.at[pl.ds(3 - 3 * (quad // 2), 3), pl.ds(6 - 6 * (quad % 2), 6)]


def token_part(ref, quad):
    return ref.at[pl.ds(3 * (quad // 2), 3), pl.ds(6 * (quad % 2), 6)]


def kernel(
    tok_hbm, kv_hbm, gain_hbm, w_qkv_hbm, table_hbm, w_proj_hbm, gout_hbm,
    key_col_hbm, key_row_hbm, skew_hbm, pick_hbm, masks_hbm, perm_hbm,
    result, grad_in, qkv_hbm, dgain_hbm, dbias_hbm,
    grad_qkv, grad_gain, grad_bias, kv, gain, w_qkv, table, w_proj, key_col, key_row, skew_ref, pick, masks, perm,
    win, fin, line_up, kvs, tabs, khs, khr, bias, allowed, dscore,
    qkvs, gms, mixs, s1, r1, s2, r2, s3, r3, ex, rx2, rx3, rx4,
    sem_in, sem_own, sem_out, sem_hs, sem_hr, sem_bs, sem_br, sem_s1, sem_r1, sem_s2, sem_r2, sem_s3, sem_r3, sem_xs, sem_xr, relay,
):
    lon, lat = lax.axis_index("lon"), lax.axis_index("lat")
    xh, zc = lax.div(lon, 32), lax.rem(lon, 32)
    z, core = lax.div(zc, 2), lax.rem(zc, 2)
    plane = xh * 8 + lat
    west, east = lax.rem(lon + N_LON - 1, N_LON), lax.rem(lon + 1, N_LON)
    north, south = lax.rem(lat + N_LAT - 1, N_LAT), lax.rem(lat + 1, N_LAT)
    twin = {"lon": lon + 1 - 2 * core, "lat": lat}
    halo_to = ({"lon": west, "lat": north}, {"lon": lon, "lat": north}, {"lon": west, "lat": lat})
    back_to = ({"lon": east, "lat": south}, {"lon": lon, "lat": south}, {"lon": east, "lat": lat})

    def plane_at(d, on=core):
        other = lax.rem(plane + d, N_PLANE)
        return other, {"lon": lax.div(other, 8) * 32 + z * 2 + on, "lat": lax.rem(other, 8)}

    def z_at(d):
        other = lax.rem(z + d, N_Z)
        return other, {"lon": xh * 32 + other * 2 + core, "lat": lat}

    def far_first(i):
        return 8 + lax.div(i, 2) * (1 - 2 * lax.rem(i, 2))

    def send(src, dst, send_sem, recv_sem, to):
        pltpu.make_async_remote_copy(
            src_ref=src, dst_ref=dst, send_sem=send_sem, recv_sem=recv_sem,
            device_id=to, device_id_type=MESH,
        ).start()

    def wait(ref, sem):
        pltpu.make_async_copy(ref, ref, sem).wait()

    barrier = pltpu.get_barrier_semaphore()

    def greet(to):
        pl.semaphore_signal(barrier, inc=1, device_id=to, device_id_type=MESH)

    def greet_both(i, carry):
        greet(plane_at(i)[1])
        greet(plane_at(i, 1 - core)[1])
        return carry

    for to in halo_to + back_to + (twin,):
        greet(to)
    for d in (4, 12, 3, 13, 2, 14, 1, 15):
        greet(z_at(d)[1])
    lax.fori_loop(1, N_PLANE, greet_both, 0)

    loads = []
    for i, (src, dst) in enumerate((
        (kv_hbm, kv), (key_col_hbm, key_col), (key_row_hbm, key_row), (table_hbm, table), (skew_hbm, skew_ref),
        (pick_hbm, pick), (masks_hbm, masks), (gain_hbm, gain), (w_qkv_hbm, w_qkv), (w_proj_hbm, w_proj), (perm_hbm, perm),
    )):
        loads.append(pltpu.make_async_copy(src, dst, sem_in.at[i]))
        loads[-1].start()
    in_kv, in_key_col, in_key_row, in_table, in_skew, in_pick, in_masks, in_gain, in_w_qkv, in_w_proj, in_perm = loads
    own = [
        pltpu.make_async_copy(token_part(ref, 3), window_part(win.at[a], 3), sem_own.at[a])
        for a, ref in enumerate((tok_hbm, gout_hbm))
    ]
    for copy in own:
        copy.start()

    pl.semaphore_wait(barrier, 45)
    for quad in range(3):
        for a, ref in enumerate((tok_hbm, gout_hbm)):
            send(token_part(ref, quad), window_part(win.at[a], quad), sem_hs.at[quad, a], sem_hr.at[quad, a], halo_to[quad])
    for d in (4, 12):
        pl.semaphore_signal(relay, inc=1, device_id=z_at(d)[1], device_id_type=MESH)

    for ready in (in_kv, in_key_col, in_key_row):
        ready.wait()
    kvs[...] = jnp.zeros_like(kvs)
    for r in range(WLAT):
        kvs[r * 2 : r * 2 + 2, 0:WLON] = kv[r].astype(F32)
    keys = dot(kvs[...].astype(BF16), key_col[...])
    for quad in range(4):
        key_line = jnp.sum(keys * key_row[quad], axis=0, keepdims=True)
        if quad == 3:
            khr[3] = key_line
        else:
            khs[quad] = key_line
            send(khs.at[quad], khr.at[quad], sem_hs.at[quad, 2], sem_hr.at[quad, 2], halo_to[quad])

    for ready in (in_table, in_skew, in_pick):
        ready.wait()
    tabs[...] = jnp.zeros_like(tabs)
    tabs[:, 0:RELN] = table[...]
    skew = jnp.broadcast_to(skew_ref[:, 0:1], (192, RELP))
    rows = jnp.concatenate(
        [jnp.broadcast_to(tabs[h : h + 1, :], (24, RELP)) for h in range(HEADS)], axis=0
    )
    rows = skewed(rows, skew, True)
    high = rows.astype(BF16)
    low = (rows - high.astype(F32)).astype(BF16)
    both = jnp.concatenate([high, low], axis=0)
    for g in range(6):
        part = dot_nt(both, pick[g])
        part = part[:192] + part[192:]
        for h in range(HEADS):
            bias[h, g * 24 : (g + 1) * 24, :] = part[h * 24 : (h + 1) * 24]

    for copy in own:
        copy.wait()
    for quad in range(3):
        for a in range(2):
            wait(window_part(win.at[a], quad), sem_hr.at[quad, a])
        wait(khr.at[quad], sem_hr.at[quad, 2])
    for ready in (in_masks, in_gain, in_w_qkv, in_w_proj, in_perm):
        ready.wait()

    def gather(a):
        line_up[...] = win[a].astype(F32).reshape(8 * 72, 128)
        levels = []
        for l in range(LEVELS):
            parts = [line_up[pl.ds(2 * j + l, 72, stride=8), :] for j in range(4)]
            levels.append(jnp.concatenate(parts, axis=1))
        return jnp.concatenate(levels, axis=0)

    x = gather(0)
    cot = gather(1)
    key_ok = (khr[0] + khr[1] + khr[2] + khr[3])[:, 0:WIN]
    edge = (lat == N_LAT - 1).astype(F32)
    allowed[...] = (1.0 - edge * masks[0]) * jnp.maximum(key_ok, masks[1])

    centred = x - jnp.mean(x, axis=-1, keepdims=True)
    spread = jnp.mean(centred * centred, axis=-1, keepdims=True)
    rstd = lax.rsqrt(spread + 1e-5)
    xhat = centred * rstd
    normed = (xhat * gain[...]).astype(BF16)
    act = dot(normed, w_qkv[...]).astype(BF16)
    grad_mixed = dot_nt(cot.astype(BF16), w_proj[...]).astype(BF16)
    for j in range(12):
        qkvs[j] = act[:, j * 128 : (j + 1) * 128]
    for j in range(4):
        gms[j] = grad_mixed[:, j * 128 : (j + 1) * 128]
    normed_t = dot_nt(perm[...], normed).astype(BF16)
    first = lax.broadcasted_iota(jnp.int32, (WIN, 128), 1) < 64

    def plane_step(p):
        wait(r1.at[p], sem_r1.at[p])
        s2[p] = (s1[p, core].astype(F32) + r1[p].astype(F32)).astype(BF16).reshape(N_PLANE, N_Z, CHUNK)

        def one(i, carry):
            d = far_first(i)
            other, to = plane_at(d)
            send(s2.at[p, other], r2.at[p, d - 1], sem_s2.at[p], sem_r2.at[p], to)
            return carry

        lax.fori_loop(1, N_PLANE, one, 0)

    def table_step(p):
        part = jnp.zeros((48, RELP), F32)
        for g in range(6):
            group = jnp.concatenate([dscore[h, g * 24 : (g + 1) * 24, :] for h in (2 * p, 2 * p + 1)], axis=0)
            part = part + dot(group.astype(BF16), pick[g])
        part = skewed(part, skew[:48], False)
        for s in range(2):
            h = 2 * p + s
            line = jnp.sum(part[s * 24 : (s + 1) * 24], axis=0, keepdims=True)
            for j in range(6):
                ex[2 * j + h // 4, h % 4 : h % 4 + 1, :] = line[:, j * 128 : (j + 1) * 128]

    ex[...] = jnp.zeros_like(ex)
    grad_normed = jnp.zeros((WIN, D), F32)
    for p in range(PAIRS):
        q2, k2, v2, gm2 = qkvs[p], qkvs[4 + p], qkvs[8 + p], gms[p]
        zero = jnp.zeros_like(q2)
        mixed = dq = dk = dv = jnp.zeros((WIN, 128), F32)
        for s in range(2):
            h = 2 * p + s
            mine = first if s == 0 else jnp.logical_not(first)
            qm = jnp.where(mine, q2, zero) * jnp.asarray(0.125, BF16)
            km = jnp.where(mine, k2, zero)
            vm = jnp.where(mine, v2, zero)
            gm = jnp.where(mine, gm2, zero)
            weights = jnp.exp(dot_nt(qm, k2) + bias[h]) * allowed[...]
            probs = weights / jnp.sum(weights, axis=-1, keepdims=True)
            attention = probs.astype(BF16)
            mixed = mixed + dot(attention, vm)
            grad_att = dot_nt(gm, v2).astype(BF16).astype(F32)
            pull = probs * grad_att
            grad_scores = pull - probs * jnp.sum(pull, axis=-1, keepdims=True)
            dscore[h] = grad_scores
            short = grad_scores.astype(BF16)
            dq = dq + dot(short, km)
            dk = dk + dot_tn(short, qm)
            dv = dv + dot_tn(attention, gm)
        mixs[:, p * 128 : (p + 1) * 128] = mixed.astype(BF16)
        act_part = jnp.concatenate([(dq * 0.125).astype(BF16), dk.astype(BF16), dv.astype(BF16)], axis=1)
        s1[p] = dot(normed_t, act_part).astype(BF16).reshape(2, 256, CHUNK)
        send(s1.at[p, 1 - core], r1.at[p], sem_s1.at[p], sem_r1.at[p], twin)
        w_part = jnp.concatenate([w_qkv[:, j * D + p * 128 : j * D + (p + 1) * 128] for j in range(3)], axis=1)
        grad_normed = grad_normed + dot_nt(act_part, w_part)
        table_step(p)
        if p > 0:
            plane_step(p - 1)

    grad_normed = grad_normed.astype(BF16).astype(F32)
    gain_part = jnp.sum(grad_normed * xhat, axis=0, keepdims=True)
    for j in range(4):
        ex[12, j : j + 1, :] = gain_part[:, j * 128 : (j + 1) * 128]
    def share_plane(i, carry):
        d = far_first(i)
        other, to = plane_at(d)
        send(ex.at[other], rx2.at[d - 1], sem_xs.at[0], sem_xr.at[0], to)
        return carry

    lax.fori_loop(1, N_PLANE, share_plane, 0)
    plane_step(PAIRS - 1)

    grad_hat = grad_normed * gain[...]
    shift = jnp.mean(grad_hat, axis=-1, keepdims=True)
    slope = jnp.mean(grad_hat * xhat, axis=-1, keepdims=True)
    dx = cot + rstd * (grad_hat - shift - xhat * slope)
    out = x + dot(mixs[...], w_proj[...]).astype(BF16).astype(F32)
    own = []
    for a, (values, ref) in enumerate(((out, result), (dx, grad_in))):
        for l in range(LEVELS):
            for j in range(4):
                line_up[pl.ds(2 * j + l, 72, stride=8), :] = values[l * 72 : (l + 1) * 72, j * 128 : (j + 1) * 128]
        fin[a] = line_up[...].reshape(WLAT, WLON, 8, 128).astype(BF16)
        for quad in range(3):
            send(window_part(fin.at[a], quad), token_part(ref, quad), sem_bs.at[quad, a], sem_br.at[quad, a], back_to[quad])
        own.append(pltpu.make_async_copy(window_part(fin.at[a], 3), token_part(ref, 3), sem_own.at[a]))
        own[-1].start()

    def z_step(p):
        wait(r2.at[p], sem_r2.at[p])
        total = s2[p, plane].astype(F32)
        for d in range(N_PLANE - 1):
            total = total + r2[p, d].astype(F32)
        for row in range(N_Z):
            s3[p, row] = total[row : row + 1]

        def one(i, carry):
            d = far_first(i)
            other, to = z_at(d)
            send(s3.at[p, other], r3.at[p, d - 1], sem_s3.at[p], sem_r3.at[p], to)
            return carry

        lax.fori_loop(1, N_Z, one, 0)

    pl.semaphore_wait(relay, 2)
    z_step(0)
    z_step(1)
    wait(rx2, sem_xr.at[0])
    rx3[z] = ex[plane] + jnp.sum(rx2[...], axis=0)

    def share_z(i, carry):
        send(rx3.at[z], rx3.at[z], sem_xs.at[1], sem_xr.at[1], z_at(far_first(i))[1])
        return carry

    lax.fori_loop(1, N_Z, share_z, 0)
    z_step(2)
    z_step(3)

    wait(rx3.at[0:15], sem_xr.at[1])
    wait(rx3.at[0:15], sem_xs.at[1])
    mine = core * N_PLANE + plane
    rx4[mine] = jnp.sum(rx3[...], axis=0)

    def share_back(i, carry):
        d = far_first(i)
        send(rx4.at[mine], rx4.at[mine], sem_xs.at[2], sem_xr.at[2], plane_at(d)[1])
        send(rx4.at[mine], rx4.at[mine], sem_xs.at[2], sem_xr.at[2], plane_at(d, 1 - core)[1])
        return carry

    lax.fori_loop(1, N_PLANE, share_back, 0)
    send(rx4.at[mine], rx4.at[mine], sem_xs.at[2], sem_xr.at[2], twin)

    for p in range(PAIRS):
        wait(r3.at[p], sem_r3.at[p])
        line = s3[p, z] + jnp.sum(r3[p], axis=0)
        for j in range(3):
            grad_qkv[:, j * D + p * 128 : j * D + (p + 1) * 128] = line[:, j * 128 : (j + 1) * 128]
    own.append(pltpu.make_async_copy(grad_qkv, qkv_hbm, sem_out.at[2]))
    own[-1].start()
    wait(rx4.at[0:31], sem_xr.at[2])
    sums = rx4[0:N_PLANE] + rx4[N_PLANE : 2 * N_PLANE]
    for j in range(4):
        grad_gain[:, j * 128 : (j + 1) * 128] = sums[12, j : j + 1, :]
    for j in range(6):
        width = min(128, RELN - j * 128)
        for half in range(2):
            grad_bias[half * 4 : half * 4 + 4, j * 128 : j * 128 + width] = sums[2 * j + half, :, 0:width]
    for i, (src, dst) in enumerate(((grad_gain, dgain_hbm), (grad_bias, dbias_hbm))):
        own.append(pltpu.make_async_copy(src, dst, sem_out.at[i]))
        own[-1].start()

    for copy in own:
        copy.wait()
    for quad in range(3):
        for a, ref in enumerate((result, grad_in)):
            wait(token_part(ref, quad), sem_br.at[quad, a])
            wait(token_part(ref, quad), sem_bs.at[quad, a])
            wait(window_part(win.at[a], quad), sem_hs.at[quad, a])
        wait(khs.at[quad], sem_hs.at[quad, 2])
    for p in range(PAIRS):
        wait(r1.at[p], sem_s1.at[p])
        wait(r2.at[p], sem_s2.at[p])
        wait(r3.at[p], sem_s3.at[p])
    wait(rx2, sem_xs.at[0])
    wait(rx4.at[0:31], sem_xs.at[2])


def finish(*refs):
    ins, outs, held, sem_in, sem_out = refs[:5], refs[5:10], refs[10:15], refs[15], refs[16]
    arrivals = [pltpu.make_async_copy(src, mid, sem_in.at[i]) for i, (src, mid) in enumerate(zip(ins, held))]
    leaves = [pltpu.make_async_copy(mid, dst, sem_out.at[i]) for i, (mid, dst) in enumerate(zip(held, outs))]
    for copy in arrivals:
        copy.start()
    for arrival, leave in zip(arrivals, leaves):
        arrival.wait()
        leave.start()
    for copy in leaves:
        copy.wait()


def to_tiles(x):
    return x.transpose(1, 2, 0, 3).reshape(WLAT, WLON, LEVELS, 4, 128).transpose(0, 1, 3, 2, 4).reshape(WLAT, WLON, 8, 128)


def from_tiles(x):
    x = x.reshape(WLAT, WLON, 4, LEVELS, 128).transpose(0, 1, 3, 2, 4).reshape(WLAT, WLON, LEVELS, D)
    return x.transpose(2, 0, 1, 3)


def local(tokens, key_valid, norm_gain, w_qkv, bias_table, w_proj, grad_out):
    hbm = pl.BlockSpec(memory_space=pl.ANY)
    tables = make_tables()
    dma = pltpu.SemaphoreType.DMA
    operands = (
        to_tiles(tokens), key_valid.transpose(1, 0, 2), norm_gain.reshape(1, D), w_qkv, bias_table, w_proj, to_tiles(grad_out),
    ) + tables
    loaded = [operands[i] for i in (1, 2, 3, 4, 5)] + list(tables)
    shapes = (
        jax.ShapeDtypeStruct((WLAT, WLON, 8, 128), BF16),
        jax.ShapeDtypeStruct((WLAT, WLON, 8, 128), BF16),
        jax.ShapeDtypeStruct((1, 3 * D), F32),
        jax.ShapeDtypeStruct((1, D), F32),
        jax.ShapeDtypeStruct((HEADS, RELN), F32),
    )
    parts = pl.pallas_call(
        kernel,
        out_shape=shapes,
        in_specs=[hbm] * len(operands),
        out_specs=[hbm] * 5,
        scratch_shapes=[pltpu.VMEM(v.shape, v.dtype) for v in list(shapes[2:]) + loaded] + [
            pltpu.VMEM((2, WLAT, WLON, 8, 128), BF16),
            pltpu.VMEM((2, WLAT, WLON, 8, 128), BF16),
            pltpu.VMEM((8 * 72, 128), F32),
            pltpu.VMEM((16, 128), F32),
            pltpu.VMEM((HEADS, RELP), F32),
            pltpu.VMEM((3, 1, 256), F32),
            pltpu.VMEM((4, 1, 256), F32),
            pltpu.VMEM((HEADS, WIN, WIN), F32),
            pltpu.VMEM((WIN, WIN), F32),
            pltpu.VMEM((HEADS, WIN, WIN), F32),
            pltpu.VMEM((12, WIN, 128), BF16),
            pltpu.VMEM((4, WIN, 128), BF16),
            pltpu.VMEM((WIN, D), BF16),
            pltpu.VMEM((PAIRS, 2, 256, CHUNK), BF16),
            pltpu.VMEM((PAIRS, 256, CHUNK), BF16),
            pltpu.VMEM((PAIRS, N_PLANE, N_Z, CHUNK), BF16),
            pltpu.VMEM((PAIRS, N_PLANE - 1, N_Z, CHUNK), BF16),
            pltpu.VMEM((PAIRS, N_Z, 1, CHUNK), F32),
            pltpu.VMEM((PAIRS, N_Z - 1, 1, CHUNK), F32),
            pltpu.VMEM((16, 4, 128), F32),
            pltpu.VMEM((15, 4, 128), F32),
            pltpu.VMEM((16, 4, 128), F32),
            pltpu.VMEM((32, 4, 128), F32),
            dma((len(loaded),)), dma((2,)), dma((3,)), dma((3, 3)), dma((3, 3)), dma((3, 2)), dma((3, 2)),
            dma((PAIRS,)), dma((PAIRS,)), dma((PAIRS,)), dma((PAIRS,)),
            dma((PAIRS,)), dma((PAIRS,)), dma((3,)), dma((3,)), pltpu.SemaphoreType.REGULAR,
        ],
        compiler_params=pltpu.CompilerParams(
            collective_id=0, has_side_effects=True, vmem_limit_bytes=VMEM_LIMIT
        ),
        name="window_block",
    )(*operands)
    result, grad_in, grad_qkv, grad_gain, grad_bias = pl.pallas_call(
        finish,
        out_shape=shapes,
        in_specs=[hbm] * 5,
        out_specs=[hbm] * 5,
        scratch_shapes=[pltpu.VMEM(v.shape, v.dtype) for v in shapes] + [dma((5,)), dma((5,))],
        compiler_params=pltpu.CompilerParams(vmem_limit_bytes=VMEM_LIMIT),
        name="finish",
    )(*parts)
    return from_tiles(result), from_tiles(grad_in), grad_qkv, grad_gain.reshape(D), grad_bias


def solution(mesh):
    placed = (
        P(None, "lat", "lon", None),
        P(None, "lat", "lon"),
        P(),
        P(),
        P(),
        P(),
        P(None, "lat", "lon", None),
    )
    return jax.shard_map(
        local,
        mesh=mesh,
        in_specs=placed,
        out_specs=(
            P(None, "lat", "lon", None),
            P(None, "lat", "lon", None),
            P(("lon", "lat"), None),
            P(),
            P(),
        ),
        check_vma=False,
    )
```

```python
import jax
import jax.numpy as jnp
import numpy as np
from jax import lax
from jax.experimental import pallas as pl
from jax.experimental.pallas import tpu as pltpu
from jax.sharding import PartitionSpec as P

MESH = pl.DeviceIdType.MESH
F32 = jnp.float32
BF16 = jnp.bfloat16

LEVELS, WLAT, WLON = 2, 6, 12
WIN = LEVELS * WLAT * WLON
D = 512
HEADS = 8
PAIRS = HEADS // 2
RELN = 759
RELP = 768
N_LON, N_LAT = 64, 8
N_Z = 16
N_PLANE = 16
CHUNK = 3 * 128
VMEM_LIMIT = 60 * 1024 * 1024


def offset_of(t):
    level, row, col = t // 72, t // 12 % 6, t % 12
    return 253 * level + 23 * row + col


def make_tables():
    key_col = np.zeros((128, 256), np.float32)
    key_row = np.zeros((4, 16, 256), np.float32)
    for l in range(LEVELS):
        for r in range(WLAT):
            for c in range(WLON):
                t = l * 72 + ((r + 3) % 6) * 12 + (c + 6) % 12
                key_col[c, t] = 1
                key_row[(r // 3) * 2 + c // 6, r * 2 + l, t] = 1
    perm = np.zeros((D, D), np.float32)
    for core in range(2):
        for xh in range(2):
            for lat in range(8):
                for z in range(16):
                    perm[core * 256 + (xh * 8 + lat) * 16 + z, xh * 256 + z * 16 + core * 8 + lat] = 1
    pick = np.zeros((6, WIN, RELP), np.float32)
    for g in range(6):
        for k in range(WIN):
            pick[g, k, (379 + 253 * (g // 3) + 46 * (g % 3) - offset_of(k)) % RELP] = 1
    step = np.arange(24)
    step = np.tile(23 * (step // 12) + step % 12, HEADS)
    skew = np.broadcast_to(step[:, None], (192, 128)).astype(np.int32)
    half = np.arange(WIN) // 12 % 6 >= 3
    masks = np.stack([half[:, None] != half[None, :], np.eye(WIN, dtype=bool)]).astype(np.float32)
    as_bf16 = lambda v: jnp.asarray(v, BF16)
    return (
        as_bf16(key_col),
        jnp.asarray(key_row),
        jnp.asarray(skew),
        as_bf16(pick),
        jnp.asarray(masks),
        as_bf16(perm),
    )


def dot(a, b):
    return lax.dot_general(a, b, (((1,), (0,)), ((), ())), preferred_element_type=F32)


def dot_nt(a, b):
    return lax.dot_general(a, b, (((1,), (1,)), ((), ())), preferred_element_type=F32)


def dot_tn(a, b):
    return lax.dot_general(a, b, (((0,), (0,)), ((), ())), preferred_element_type=F32)


def skewed(rows, skew, left):
    for bit in (1, 2, 4, 8, 16, 32):
        moved = pltpu.roll(rows, RELP - bit if left else bit, 1)
        rows = jnp.where((skew & bit) != 0, moved, rows)
    return rows


def window_part(ref, quad):
    return ref.at[pl.ds(3 - 3 * (quad // 2), 3), pl.ds(6 - 6 * (quad % 2), 6)]


def token_part(ref, quad):
    return ref.at[pl.ds(3 * (quad // 2), 3), pl.ds(6 * (quad % 2), 6)]


def kernel(
    tok_hbm, kv_hbm, gain_hbm, w_qkv_hbm, table_hbm, w_proj_hbm, gout_hbm,
    key_col_hbm, key_row_hbm, skew_hbm, pick_hbm, masks_hbm, perm_hbm,
    result, grad_in, qkv_hbm, dgain_hbm, dbias_hbm,
    grad_qkv, grad_gain, grad_bias, kv, gain, w_qkv, table, w_proj, key_col, key_row, skew_ref, pick, masks, perm,
    win, fin, line_up, kvs, tabs, khs, khr, bias, allowed, dscore,
    qkvs, gms, mixs, s1, r1, s2, r2, s3, r3, ex, rx2, rx3, rx4,
    sem_in, sem_own, sem_out, sem_hs, sem_hr, sem_bs, sem_br, sem_s1, sem_r1, sem_s2, sem_r2, sem_s3, sem_r3, sem_xs, sem_xr, relay,
):
    lon, lat = lax.axis_index("lon"), lax.axis_index("lat")
    xh, zc = lax.div(lon, 32), lax.rem(lon, 32)
    z, core = lax.div(zc, 2), lax.rem(zc, 2)
    plane = xh * 8 + lat
    x_at, y_at = lax.div(plane, 4), lax.rem(plane, 4)
    west, east = lax.rem(lon + N_LON - 1, N_LON), lax.rem(lon + 1, N_LON)
    north, south = lax.rem(lat + N_LAT - 1, N_LAT), lax.rem(lat + 1, N_LAT)
    twin = {"lon": lon + 1 - 2 * core, "lat": lat}
    halo_to = ({"lon": west, "lat": north}, {"lon": lon, "lat": north}, {"lon": west, "lat": lat})
    back_to = ({"lon": east, "lat": south}, {"lon": lon, "lat": south}, {"lon": east, "lat": lat})

    def plane_at(d, on=core):
        slow, fast = lax.div(d, 4), lax.rem(d, 4)
        x_to = lax.rem(x_at + slow + core * (fast - slow), 4)
        y_to = lax.rem(y_at + fast + core * (slow - fast), 4)
        other = x_to * 4 + y_to
        return other, {"lon": lax.div(x_to, 2) * 32 + z * 2 + on, "lat": lax.rem(x_to, 2) * 4 + y_to}

    def z_at(d):
        other = lax.rem(z + d, N_Z)
        return other, {"lon": xh * 32 + other * 2 + core, "lat": lat}

    def far_first(i):
        return 8 + lax.div(i, 2) * (1 - 2 * lax.rem(i, 2))

    def send(src, dst, send_sem, recv_sem, to):
        pltpu.make_async_remote_copy(
            src_ref=src, dst_ref=dst, send_sem=send_sem, recv_sem=recv_sem,
            device_id=to, device_id_type=MESH,
        ).start()

    def wait(ref, sem):
        pltpu.make_async_copy(ref, ref, sem).wait()

    barrier = pltpu.get_barrier_semaphore()

    def greet(to):
        pl.semaphore_signal(barrier, inc=1, device_id=to, device_id_type=MESH)

    def greet_both(i, carry):
        greet(plane_at(i)[1])
        greet(plane_at(i, 1 - core)[1])
        return carry

    for to in halo_to + back_to + (twin,):
        greet(to)
    for d in (4, 12, 3, 13, 2, 14, 1, 15):
        greet(z_at(d)[1])
    lax.fori_loop(1, N_PLANE, greet_both, 0)

    loads = []
    for i, (src, dst) in enumerate((
        (kv_hbm, kv), (key_col_hbm, key_col), (key_row_hbm, key_row), (table_hbm, table), (skew_hbm, skew_ref),
        (pick_hbm, pick), (masks_hbm, masks), (gain_hbm, gain), (w_qkv_hbm, w_qkv), (w_proj_hbm, w_proj), (perm_hbm, perm),
    )):
        loads.append(pltpu.make_async_copy(src, dst, sem_in.at[i]))
        loads[-1].start()
    in_kv, in_key_col, in_key_row, in_table, in_skew, in_pick, in_masks, in_gain, in_w_qkv, in_w_proj, in_perm = loads
    own = [
        pltpu.make_async_copy(token_part(ref, 3), window_part(win.at[a], 3), sem_own.at[a])
        for a, ref in enumerate((tok_hbm, gout_hbm))
    ]
    for copy in own:
        copy.start()

    pl.semaphore_wait(barrier, 45)
    for quad in range(3):
        for a, ref in enumerate((tok_hbm, gout_hbm)):
            send(token_part(ref, quad), window_part(win.at[a], quad), sem_hs.at[quad, a], sem_hr.at[quad, a], halo_to[quad])
    for d in (4, 12):
        pl.semaphore_signal(relay, inc=1, device_id=z_at(d)[1], device_id_type=MESH)

    for ready in (in_kv, in_key_col, in_key_row):
        ready.wait()
    kvs[...] = jnp.zeros_like(kvs)
    for r in range(WLAT):
        kvs[r * 2 : r * 2 + 2, 0:WLON] = kv[r].astype(F32)
    keys = dot(kvs[...].astype(BF16), key_col[...])
    for quad in range(4):
        key_line = jnp.sum(keys * key_row[quad], axis=0, keepdims=True)
        if quad == 3:
            khr[3] = key_line
        else:
            khs[quad] = key_line
            send(khs.at[quad], khr.at[quad], sem_hs.at[quad, 2], sem_hr.at[quad, 2], halo_to[quad])

    for ready in (in_table, in_skew, in_pick):
        ready.wait()
    tabs[...] = jnp.zeros_like(tabs)
    tabs[:, 0:RELN] = table[...]
    skew = jnp.broadcast_to(skew_ref[:, 0:1], (192, RELP))
    rows = jnp.concatenate(
        [jnp.broadcast_to(tabs[h : h + 1, :], (24, RELP)) for h in range(HEADS)], axis=0
    )
    rows = skewed(rows, skew, True)
    high = rows.astype(BF16)
    low = (rows - high.astype(F32)).astype(BF16)
    both = jnp.concatenate([high, low], axis=0)
    for g in range(6):
        part = dot_nt(both, pick[g])
        part = part[:192] + part[192:]
        for h in range(HEADS):
            bias[h, g * 24 : (g + 1) * 24, :] = part[h * 24 : (h + 1) * 24]

    for copy in own:
        copy.wait()
    for quad in range(3):
        for a in range(2):
            wait(window_part(win.at[a], quad), sem_hr.at[quad, a])
        wait(khr.at[quad], sem_hr.at[quad, 2])
    for ready in (in_masks, in_gain, in_w_qkv, in_w_proj, in_perm):
        ready.wait()

    def gather(a):
        line_up[...] = win[a].astype(F32).reshape(8 * 72, 128)
        levels = []
        for l in range(LEVELS):
            parts = [line_up[pl.ds(2 * j + l, 72, stride=8), :] for j in range(4)]
            levels.append(jnp.concatenate(parts, axis=1))
        return jnp.concatenate(levels, axis=0)

    x = gather(0)
    cot = gather(1)
    key_ok = (khr[0] + khr[1] + khr[2] + khr[3])[:, 0:WIN]
    edge = (lat == N_LAT - 1).astype(F32)
    allowed[...] = (1.0 - edge * masks[0]) * jnp.maximum(key_ok, masks[1])

    centred = x - jnp.mean(x, axis=-1, keepdims=True)
    spread = jnp.mean(centred * centred, axis=-1, keepdims=True)
    rstd = lax.rsqrt(spread + 1e-5)
    xhat = centred * rstd
    normed = (xhat * gain[...]).astype(BF16)
    act = dot(normed, w_qkv[...]).astype(BF16)
    grad_mixed = dot_nt(cot.astype(BF16), w_proj[...]).astype(BF16)
    for j in range(12):
        qkvs[j] = act[:, j * 128 : (j + 1) * 128]
    for j in range(4):
        gms[j] = grad_mixed[:, j * 128 : (j + 1) * 128]
    normed_t = dot_nt(perm[...], normed).astype(BF16)
    first = lax.broadcasted_iota(jnp.int32, (WIN, 128), 1) < 64

    def plane_step(p):
        wait(r1.at[p], sem_r1.at[p])
        s2[p] = (s1[p, core].astype(F32) + r1[p].astype(F32)).astype(BF16).reshape(N_PLANE, N_Z, CHUNK)

        def one(i, carry):
            d = far_first(i)
            other, to = plane_at(d)
            send(s2.at[p, other], r2.at[p, d - 1], sem_s2.at[p], sem_r2.at[p], to)
            return carry

        lax.fori_loop(1, N_PLANE, one, 0)

    def table_step(p):
        part = jnp.zeros((48, RELP), F32)
        for g in range(6):
            group = jnp.concatenate([dscore[h, g * 24 : (g + 1) * 24, :] for h in (2 * p, 2 * p + 1)], axis=0)
            part = part + dot(group.astype(BF16), pick[g])
        part = skewed(part, skew[:48], False)
        for s in range(2):
            h = 2 * p + s
            line = jnp.sum(part[s * 24 : (s + 1) * 24], axis=0, keepdims=True)
            for j in range(6):
                ex[2 * j + h // 4, h % 4 : h % 4 + 1, :] = line[:, j * 128 : (j + 1) * 128]

    ex[...] = jnp.zeros_like(ex)
    grad_normed = jnp.zeros((WIN, D), F32)
    for p in range(PAIRS):
        q2, k2, v2, gm2 = qkvs[p], qkvs[4 + p], qkvs[8 + p], gms[p]
        zero = jnp.zeros_like(q2)
        mixed = dq = dk = dv = jnp.zeros((WIN, 128), F32)
        for s in range(2):
            h = 2 * p + s
            mine = first if s == 0 else jnp.logical_not(first)
            qm = jnp.where(mine, q2, zero) * jnp.asarray(0.125, BF16)
            km = jnp.where(mine, k2, zero)
            vm = jnp.where(mine, v2, zero)
            gm = jnp.where(mine, gm2, zero)
            weights = jnp.exp(dot_nt(qm, k2) + bias[h]) * allowed[...]
            probs = weights / jnp.sum(weights, axis=-1, keepdims=True)
            attention = probs.astype(BF16)
            mixed = mixed + dot(attention, vm)
            grad_att = dot_nt(gm, v2).astype(BF16).astype(F32)
            pull = probs * grad_att
            grad_scores = pull - probs * jnp.sum(pull, axis=-1, keepdims=True)
            dscore[h] = grad_scores
            short = grad_scores.astype(BF16)
            dq = dq + dot(short, km)
            dk = dk + dot_tn(short, qm)
            dv = dv + dot_tn(attention, gm)
            if s == 0 and 0 < p < PAIRS - 1:
                plane_step(p - 1)
        mixs[:, p * 128 : (p + 1) * 128] = mixed.astype(BF16)
        act_part = jnp.concatenate([(dq * 0.125).astype(BF16), dk.astype(BF16), dv.astype(BF16)], axis=1)
        s1[p] = dot(normed_t, act_part).astype(BF16).reshape(2, 256, CHUNK)
        send(s1.at[p, 1 - core], r1.at[p], sem_s1.at[p], sem_r1.at[p], twin)
        w_part = jnp.concatenate([w_qkv[:, j * D + p * 128 : j * D + (p + 1) * 128] for j in range(3)], axis=1)
        grad_normed = grad_normed + dot_nt(act_part, w_part)
        table_step(p)

    grad_normed = grad_normed.astype(BF16).astype(F32)
    gain_part = jnp.sum(grad_normed * xhat, axis=0, keepdims=True)
    for j in range(4):
        ex[12, j : j + 1, :] = gain_part[:, j * 128 : (j + 1) * 128]
    def share_plane(i, carry):
        d = far_first(i)
        other, to = plane_at(d)
        send(ex.at[other], rx2.at[d - 1], sem_xs.at[0], sem_xr.at[0], to)
        return carry

    lax.fori_loop(1, N_PLANE, share_plane, 0)
    plane_step(PAIRS - 2)
    plane_step(PAIRS - 1)

    grad_hat = grad_normed * gain[...]
    shift = jnp.mean(grad_hat, axis=-1, keepdims=True)
    slope = jnp.mean(grad_hat * xhat, axis=-1, keepdims=True)
    dx = cot + rstd * (grad_hat - shift - xhat * slope)
    out = x + dot(mixs[...], w_proj[...]).astype(BF16).astype(F32)
    own = []
    for a, (values, ref) in enumerate(((out, result), (dx, grad_in))):
        for l in range(LEVELS):
            for j in range(4):
                line_up[pl.ds(2 * j + l, 72, stride=8), :] = values[l * 72 : (l + 1) * 72, j * 128 : (j + 1) * 128]
        fin[a] = line_up[...].reshape(WLAT, WLON, 8, 128).astype(BF16)
        for quad in range(3):
            send(window_part(fin.at[a], quad), token_part(ref, quad), sem_bs.at[quad, a], sem_br.at[quad, a], back_to[quad])
        own.append(pltpu.make_async_copy(window_part(fin.at[a], 3), token_part(ref, 3), sem_own.at[a]))
        own[-1].start()

    def z_step(p):
        wait(r2.at[p], sem_r2.at[p])
        total = s2[p, plane].astype(F32)
        for d in range(N_PLANE - 1):
            total = total + r2[p, d].astype(F32)
        for row in range(N_Z):
            s3[p, row] = total[row : row + 1]

        def one(i, carry):
            d = far_first(i)
            other, to = z_at(d)
            send(s3.at[p, other], r3.at[p, d - 1], sem_s3.at[p], sem_r3.at[p], to)
            return carry

        lax.fori_loop(1, N_Z, one, 0)

    pl.semaphore_wait(relay, 2)
    wait(rx2, sem_xr.at[0])
    rx3[z] = ex[plane] + jnp.sum(rx2[...], axis=0)

    def share_z(i, carry):
        send(rx3.at[z], rx3.at[z], sem_xs.at[1], sem_xr.at[1], z_at(far_first(i))[1])
        return carry

    lax.fori_loop(1, N_Z, share_z, 0)
    for p in range(PAIRS):
        z_step(p)

    wait(rx3.at[0:15], sem_xr.at[1])
    wait(rx3.at[0:15], sem_xs.at[1])
    mine = core * N_PLANE + plane
    rx4[mine] = jnp.sum(rx3[...], axis=0)

    def share_back(i, carry):
        d = far_first(i)
        send(rx4.at[mine], rx4.at[mine], sem_xs.at[2], sem_xr.at[2], plane_at(d)[1])
        send(rx4.at[mine], rx4.at[mine], sem_xs.at[2], sem_xr.at[2], plane_at(d, 1 - core)[1])
        return carry

    lax.fori_loop(1, N_PLANE, share_back, 0)
    send(rx4.at[mine], rx4.at[mine], sem_xs.at[2], sem_xr.at[2], twin)

    for p in range(PAIRS):
        wait(r3.at[p], sem_r3.at[p])
        line = s3[p, z] + jnp.sum(r3[p], axis=0)
        for j in range(3):
            grad_qkv[:, j * D + p * 128 : j * D + (p + 1) * 128] = line[:, j * 128 : (j + 1) * 128]
    own.append(pltpu.make_async_copy(grad_qkv, qkv_hbm, sem_out.at[2]))
    own[-1].start()
    wait(rx4.at[0:31], sem_xr.at[2])
    sums = rx4[0:N_PLANE] + rx4[N_PLANE : 2 * N_PLANE]
    for j in range(4):
        grad_gain[:, j * 128 : (j + 1) * 128] = sums[12, j : j + 1, :]
    for j in range(6):
        width = min(128, RELN - j * 128)
        for half in range(2):
            grad_bias[half * 4 : half * 4 + 4, j * 128 : j * 128 + width] = sums[2 * j + half, :, 0:width]
    for i, (src, dst) in enumerate(((grad_gain, dgain_hbm), (grad_bias, dbias_hbm))):
        own.append(pltpu.make_async_copy(src, dst, sem_out.at[i]))
        own[-1].start()

    for copy in own:
        copy.wait()
    for quad in range(3):
        for a, ref in enumerate((result, grad_in)):
            wait(token_part(ref, quad), sem_br.at[quad, a])
            wait(token_part(ref, quad), sem_bs.at[quad, a])
            wait(window_part(win.at[a], quad), sem_hs.at[quad, a])
        wait(khs.at[quad], sem_hs.at[quad, 2])
    for p in range(PAIRS):
        wait(r1.at[p], sem_s1.at[p])
        wait(r2.at[p], sem_s2.at[p])
        wait(r3.at[p], sem_s3.at[p])
    wait(rx2, sem_xs.at[0])
    wait(rx4.at[0:31], sem_xs.at[2])


def finish(*refs):
    ins, outs, held, sem_in, sem_out = refs[:5], refs[5:10], refs[10:15], refs[15], refs[16]
    arrivals = [pltpu.make_async_copy(src, mid, sem_in.at[i]) for i, (src, mid) in enumerate(zip(ins, held))]
    leaves = [pltpu.make_async_copy(mid, dst, sem_out.at[i]) for i, (mid, dst) in enumerate(zip(held, outs))]
    for copy in arrivals:
        copy.start()
    for arrival, leave in zip(arrivals, leaves):
        arrival.wait()
        leave.start()
    for copy in leaves:
        copy.wait()


def to_tiles(x):
    return x.transpose(1, 2, 0, 3).reshape(WLAT, WLON, LEVELS, 4, 128).transpose(0, 1, 3, 2, 4).reshape(WLAT, WLON, 8, 128)


def from_tiles(x):
    x = x.reshape(WLAT, WLON, 4, LEVELS, 128).transpose(0, 1, 3, 2, 4).reshape(WLAT, WLON, LEVELS, D)
    return x.transpose(2, 0, 1, 3)


def local(tokens, key_valid, norm_gain, w_qkv, bias_table, w_proj, grad_out):
    hbm = pl.BlockSpec(memory_space=pl.ANY)
    tables = make_tables()
    dma = pltpu.SemaphoreType.DMA
    operands = (
        to_tiles(tokens), key_valid.transpose(1, 0, 2), norm_gain.reshape(1, D), w_qkv, bias_table, w_proj, to_tiles(grad_out),
    ) + tables
    loaded = [operands[i] for i in (1, 2, 3, 4, 5)] + list(tables)
    shapes = (
        jax.ShapeDtypeStruct((WLAT, WLON, 8, 128), BF16),
        jax.ShapeDtypeStruct((WLAT, WLON, 8, 128), BF16),
        jax.ShapeDtypeStruct((1, 3 * D), F32),
        jax.ShapeDtypeStruct((1, D), F32),
        jax.ShapeDtypeStruct((HEADS, RELN), F32),
    )
    parts = pl.pallas_call(
        kernel,
        out_shape=shapes,
        in_specs=[hbm] * len(operands),
        out_specs=[hbm] * 5,
        scratch_shapes=[pltpu.VMEM(v.shape, v.dtype) for v in list(shapes[2:]) + loaded] + [
            pltpu.VMEM((2, WLAT, WLON, 8, 128), BF16),
            pltpu.VMEM((2, WLAT, WLON, 8, 128), BF16),
            pltpu.VMEM((8 * 72, 128), F32),
            pltpu.VMEM((16, 128), F32),
            pltpu.VMEM((HEADS, RELP), F32),
            pltpu.VMEM((3, 1, 256), F32),
            pltpu.VMEM((4, 1, 256), F32),
            pltpu.VMEM((HEADS, WIN, WIN), F32),
            pltpu.VMEM((WIN, WIN), F32),
            pltpu.VMEM((HEADS, WIN, WIN), F32),
            pltpu.VMEM((12, WIN, 128), BF16),
            pltpu.VMEM((4, WIN, 128), BF16),
            pltpu.VMEM((WIN, D), BF16),
            pltpu.VMEM((PAIRS, 2, 256, CHUNK), BF16),
            pltpu.VMEM((PAIRS, 256, CHUNK), BF16),
            pltpu.VMEM((PAIRS, N_PLANE, N_Z, CHUNK), BF16),
            pltpu.VMEM((PAIRS, N_PLANE - 1, N_Z, CHUNK), BF16),
            pltpu.VMEM((PAIRS, N_Z, 1, CHUNK), F32),
            pltpu.VMEM((PAIRS, N_Z - 1, 1, CHUNK), F32),
            pltpu.VMEM((16, 4, 128), F32),
            pltpu.VMEM((15, 4, 128), F32),
            pltpu.VMEM((16, 4, 128), F32),
            pltpu.VMEM((32, 4, 128), F32),
            dma((len(loaded),)), dma((2,)), dma((3,)), dma((3, 3)), dma((3, 3)), dma((3, 2)), dma((3, 2)),
            dma((PAIRS,)), dma((PAIRS,)), dma((PAIRS,)), dma((PAIRS,)),
            dma((PAIRS,)), dma((PAIRS,)), dma((3,)), dma((3,)), pltpu.SemaphoreType.REGULAR,
        ],
        compiler_params=pltpu.CompilerParams(
            collective_id=0, has_side_effects=True, vmem_limit_bytes=VMEM_LIMIT
        ),
        name="window_block",
    )(*operands)
    result, grad_in, grad_qkv, grad_gain, grad_bias = pl.pallas_call(
        finish,
        out_shape=shapes,
        in_specs=[hbm] * 5,
        out_specs=[hbm] * 5,
        scratch_shapes=[pltpu.VMEM(v.shape, v.dtype) for v in shapes] + [dma((5,)), dma((5,))],
        compiler_params=pltpu.CompilerParams(vmem_limit_bytes=VMEM_LIMIT),
        name="finish",
    )(*parts)
    return from_tiles(result), from_tiles(grad_in), grad_qkv, grad_gain.reshape(D), grad_bias


def solution(mesh):
    placed = (
        P(None, "lat", "lon", None),
        P(None, "lat", "lon"),
        P(),
        P(),
        P(),
        P(),
        P(None, "lat", "lon", None),
    )
    return jax.shard_map(
        local,
        mesh=mesh,
        in_specs=placed,
        out_specs=(
            P(None, "lat", "lon", None),
            P(None, "lat", "lon", None),
            P(("lon", "lat"), None),
            P(),
            P(),
        ),
        check_vma=False,
    )
```

```python
import jax
import jax.numpy as jnp
import numpy as np
from jax import lax
from jax.experimental import pallas as pl
from jax.experimental.pallas import tpu as pltpu
from jax.sharding import PartitionSpec as P

MESH = pl.DeviceIdType.MESH
F32 = jnp.float32
BF16 = jnp.bfloat16

LEVELS, WLAT, WLON = 2, 6, 12
WIN = LEVELS * WLAT * WLON
D = 512
HEADS = 8
PAIRS = HEADS // 2
RELN = 759
RELP = 768
N_LON, N_LAT = 64, 8
N_Z = 16
N_PLANE = 16
CHUNK = 3 * 128
VMEM_LIMIT = 60 * 1024 * 1024


def offset_of(t):
    level, row, col = t // 72, t // 12 % 6, t % 12
    return 253 * level + 23 * row + col


def make_tables():
    key_col = np.zeros((128, 256), np.float32)
    key_row = np.zeros((4, 16, 256), np.float32)
    for l in range(LEVELS):
        for r in range(WLAT):
            for c in range(WLON):
                t = l * 72 + ((r + 3) % 6) * 12 + (c + 6) % 12
                key_col[c, t] = 1
                key_row[(r // 3) * 2 + c // 6, r * 2 + l, t] = 1
    perm = np.zeros((D, D), np.float32)
    for core in range(2):
        for xh in range(2):
            for lat in range(8):
                for z in range(16):
                    perm[core * 256 + (xh * 8 + lat) * 16 + z, xh * 256 + z * 16 + core * 8 + lat] = 1
    pick = np.zeros((6, WIN, RELP), np.float32)
    for g in range(6):
        for k in range(WIN):
            pick[g, k, (379 + 253 * (g // 3) + 46 * (g % 3) - offset_of(k)) % RELP] = 1
    step = np.arange(24)
    step = np.tile(23 * (step // 12) + step % 12, HEADS)
    skew = np.broadcast_to(step[:, None], (192, 128)).astype(np.int32)
    half = np.arange(WIN) // 12 % 6 >= 3
    masks = np.stack([half[:, None] != half[None, :], np.eye(WIN, dtype=bool)]).astype(np.float32)
    as_bf16 = lambda v: jnp.asarray(v, BF16)
    return (
        as_bf16(key_col),
        jnp.asarray(key_row),
        jnp.asarray(skew),
        as_bf16(pick),
        jnp.asarray(masks),
        as_bf16(perm),
    )


def dot(a, b):
    return lax.dot_general(a, b, (((1,), (0,)), ((), ())), preferred_element_type=F32)


def dot_nt(a, b):
    return lax.dot_general(a, b, (((1,), (1,)), ((), ())), preferred_element_type=F32)


def dot_tn(a, b):
    return lax.dot_general(a, b, (((0,), (0,)), ((), ())), preferred_element_type=F32)


def skewed(rows, skew, left):
    for bit in (1, 2, 4, 8, 16, 32):
        moved = pltpu.roll(rows, RELP - bit if left else bit, 1)
        rows = jnp.where((skew & bit) != 0, moved, rows)
    return rows


def window_part(ref, quad):
    return ref.at[pl.ds(3 - 3 * (quad // 2), 3), pl.ds(6 - 6 * (quad % 2), 6)]


def token_part(ref, quad):
    return ref.at[pl.ds(3 * (quad // 2), 3), pl.ds(6 * (quad % 2), 6)]


def kernel(
    tok_hbm, kv_hbm, gain_hbm, w_qkv_hbm, table_hbm, w_proj_hbm, gout_hbm,
    key_col_hbm, key_row_hbm, skew_hbm, pick_hbm, masks_hbm, perm_hbm,
    result, grad_in, qkv_hbm, dgain_hbm, dbias_hbm,
    grad_qkv, grad_gain, grad_bias, kv, gain, w_qkv, table, w_proj, key_col, key_row, skew_ref, pick, masks, perm,
    win, fin, line_up, kvs, tabs, khs, khr, bias, allowed, dscore,
    qkvs, gms, mixs, s1, r1, s2, r2, s3, r3, ex, rx2, rx3, rx4,
    sem_in, sem_own, sem_out, sem_hs, sem_hr, sem_bs, sem_br, sem_s1, sem_r1, sem_s2, sem_r2, sem_s3, sem_r3, sem_xs, sem_xr, relay,
):
    lon, lat = lax.axis_index("lon"), lax.axis_index("lat")
    xh, zc = lax.div(lon, 32), lax.rem(lon, 32)
    z, core = lax.div(zc, 2), lax.rem(zc, 2)
    plane = xh * 8 + lat
    x_at, y_at = lax.div(plane, 4), lax.rem(plane, 4)
    west, east = lax.rem(lon + N_LON - 1, N_LON), lax.rem(lon + 1, N_LON)
    north, south = lax.rem(lat + N_LAT - 1, N_LAT), lax.rem(lat + 1, N_LAT)
    twin = {"lon": lon + 1 - 2 * core, "lat": lat}
    halo_to = ({"lon": west, "lat": north}, {"lon": lon, "lat": north}, {"lon": west, "lat": lat})
    back_to = ({"lon": east, "lat": south}, {"lon": lon, "lat": south}, {"lon": east, "lat": lat})

    def plane_at(d, on=core):
        slow, fast = lax.div(d, 4), lax.rem(d, 4)
        x_to = lax.rem(x_at + slow + core * (fast - slow), 4)
        y_to = lax.rem(y_at + fast + core * (slow - fast), 4)
        other = x_to * 4 + y_to
        return other, {"lon": lax.div(x_to, 2) * 32 + z * 2 + on, "lat": lax.rem(x_to, 2) * 4 + y_to}

    def z_at(d):
        other = lax.rem(z + d, N_Z)
        return other, {"lon": xh * 32 + other * 2 + core, "lat": lat}

    def far_first(i):
        return 8 + lax.div(i, 2) * (1 - 2 * lax.rem(i, 2))

    def send(src, dst, send_sem, recv_sem, to):
        pltpu.make_async_remote_copy(
            src_ref=src, dst_ref=dst, send_sem=send_sem, recv_sem=recv_sem,
            device_id=to, device_id_type=MESH,
        ).start()

    def wait(ref, sem):
        pltpu.make_async_copy(ref, ref, sem).wait()

    barrier = pltpu.get_barrier_semaphore()

    def greet(to):
        pl.semaphore_signal(barrier, inc=1, device_id=to, device_id_type=MESH)

    def greet_both(i, carry):
        greet(plane_at(i)[1])
        greet(plane_at(i, 1 - core)[1])
        return carry

    for to in halo_to + back_to + (twin,):
        greet(to)
    for d in (4, 12, 3, 13, 2, 14, 1, 15):
        greet(z_at(d)[1])
    lax.fori_loop(1, N_PLANE, greet_both, 0)

    loads = []
    for i, (src, dst) in enumerate((
        (kv_hbm, kv), (key_col_hbm, key_col), (key_row_hbm, key_row), (table_hbm, table), (skew_hbm, skew_ref),
        (pick_hbm, pick), (masks_hbm, masks), (gain_hbm, gain), (w_qkv_hbm, w_qkv), (w_proj_hbm, w_proj), (perm_hbm, perm),
    )):
        loads.append(pltpu.make_async_copy(src, dst, sem_in.at[i]))
        loads[-1].start()
    in_kv, in_key_col, in_key_row, in_table, in_skew, in_pick, in_masks, in_gain, in_w_qkv, in_w_proj, in_perm = loads
    own = [
        pltpu.make_async_copy(token_part(ref, 3), window_part(win.at[a], 3), sem_own.at[a])
        for a, ref in enumerate((tok_hbm, gout_hbm))
    ]
    for copy in own:
        copy.start()

    pl.semaphore_wait(barrier, 45)
    for quad in range(3):
        for a, ref in enumerate((tok_hbm, gout_hbm)):
            send(token_part(ref, quad), window_part(win.at[a], quad), sem_hs.at[quad, a], sem_hr.at[quad, a], halo_to[quad])
    for d in (4, 12):
        pl.semaphore_signal(relay, inc=1, device_id=z_at(d)[1], device_id_type=MESH)

    for ready in (in_kv, in_key_col, in_key_row):
        ready.wait()
    kvs[...] = jnp.zeros_like(kvs)
    for r in range(WLAT):
        kvs[r * 2 : r * 2 + 2, 0:WLON] = kv[r].astype(F32)
    keys = dot(kvs[...].astype(BF16), key_col[...])
    for quad in range(4):
        key_line = jnp.sum(keys * key_row[quad], axis=0, keepdims=True)
        if quad == 3:
            khr[3] = key_line
        else:
            khs[quad] = key_line
            send(khs.at[quad], khr.at[quad], sem_hs.at[quad, 2], sem_hr.at[quad, 2], halo_to[quad])

    for ready in (in_table, in_skew, in_pick):
        ready.wait()
    tabs[...] = jnp.zeros_like(tabs)
    tabs[:, 0:RELN] = table[...]
    skew = jnp.broadcast_to(skew_ref[:, 0:1], (192, RELP))
    rows = jnp.concatenate(
        [jnp.broadcast_to(tabs[h : h + 1, :], (24, RELP)) for h in range(HEADS)], axis=0
    )
    rows = skewed(rows, skew, True)
    high = rows.astype(BF16)
    low = (rows - high.astype(F32)).astype(BF16)
    both = jnp.concatenate([high, low], axis=0)
    for g in range(6):
        part = dot_nt(both, pick[g])
        part = part[:192] + part[192:]
        for h in range(HEADS):
            bias[h, g * 24 : (g + 1) * 24, :] = part[h * 24 : (h + 1) * 24]

    for copy in own:
        copy.wait()
    for quad in range(3):
        for a in range(2):
            wait(window_part(win.at[a], quad), sem_hr.at[quad, a])
        wait(khr.at[quad], sem_hr.at[quad, 2])
    for ready in (in_masks, in_gain, in_w_qkv, in_w_proj, in_perm):
        ready.wait()

    def gather(a):
        line_up[...] = win[a].astype(F32).reshape(8 * 72, 128)
        levels = []
        for l in range(LEVELS):
            parts = [line_up[pl.ds(2 * j + l, 72, stride=8), :] for j in range(4)]
            levels.append(jnp.concatenate(parts, axis=1))
        return jnp.concatenate(levels, axis=0)

    x = gather(0)
    cot = gather(1)
    key_ok = (khr[0] + khr[1] + khr[2] + khr[3])[:, 0:WIN]
    edge = (lat == N_LAT - 1).astype(F32)
    allowed[...] = (1.0 - edge * masks[0]) * jnp.maximum(key_ok, masks[1])

    centred = x - jnp.mean(x, axis=-1, keepdims=True)
    spread = jnp.mean(centred * centred, axis=-1, keepdims=True)
    rstd = lax.rsqrt(spread + 1e-5)
    xhat = centred * rstd
    normed = (xhat * gain[...]).astype(BF16)
    act = dot(normed, w_qkv[...]).astype(BF16)
    grad_mixed = dot_nt(cot.astype(BF16), w_proj[...]).astype(BF16)
    for j in range(12):
        qkvs[j] = act[:, j * 128 : (j + 1) * 128]
    for j in range(4):
        gms[j] = grad_mixed[:, j * 128 : (j + 1) * 128]
    normed_t = dot_nt(perm[...], normed).astype(BF16)
    first = lax.broadcasted_iota(jnp.int32, (WIN, 128), 1) < 64

    def plane_step(p):
        wait(r1.at[p], sem_r1.at[p])
        s2[p] = (s1[p, core].astype(F32) + r1[p].astype(F32)).astype(BF16).reshape(N_PLANE, N_Z, CHUNK)

        def one(i, carry):
            d = far_first(i)
            other, to = plane_at(d)
            send(s2.at[p, other], r2.at[p, d - 1], sem_s2.at[p], sem_r2.at[p], to)
            return carry

        lax.fori_loop(1, N_PLANE, one, 0)

    def table_step(heads):
        part = jnp.zeros((24 * len(heads), RELP), F32)
        for g in range(6):
            group = jnp.concatenate([dscore[h, g * 24 : (g + 1) * 24, :] for h in heads], axis=0)
            part = part + dot(group.astype(BF16), pick[g])
        part = skewed(part, skew[: 24 * len(heads)], False)
        for s, h in enumerate(heads):
            line = jnp.sum(part[s * 24 : (s + 1) * 24], axis=0, keepdims=True)
            for j in range(6):
                ex[2 * j + h // 4, h % 4 : h % 4 + 1, :] = line[:, j * 128 : (j + 1) * 128]

    ex[...] = jnp.zeros_like(ex)
    grad_normed = jnp.zeros((WIN, D), F32)
    for p in range(PAIRS):
        q2, k2, v2, gm2 = qkvs[p], qkvs[4 + p], qkvs[8 + p], gms[p]
        zero = jnp.zeros_like(q2)
        mixed = dq = jnp.zeros((WIN, 128), F32)
        q_t, gm_t = (q2 * jnp.asarray(0.125, BF16)).T, gm2.T
        dk_t, dv_t = [], []
        for s in range(2):
            h = 2 * p + s
            mine = first if s == 0 else jnp.logical_not(first)
            qm = jnp.where(mine, q2, zero) * jnp.asarray(0.125, BF16)
            km = jnp.where(mine, k2, zero)
            vm = jnp.where(mine, v2, zero)
            gm = jnp.where(mine, gm2, zero)
            weights = jnp.exp(dot_nt(qm, k2) + bias[h]) * allowed[...]
            probs = weights * (1.0 / jnp.sum(weights, axis=-1, keepdims=True))
            attention = probs.astype(BF16)
            mixed = mixed + dot(attention, vm)
            grad_att = dot_nt(gm, v2).astype(BF16).astype(F32)
            pull = probs * grad_att
            grad_scores = pull - probs * jnp.sum(pull, axis=-1, keepdims=True)
            dscore[h] = grad_scores
            short = grad_scores.astype(BF16)
            dq = dq + dot(short, km)
            dk_t.append(dot(q_t[s * 64 : (s + 1) * 64], short))
            dv_t.append(dot(gm_t[s * 64 : (s + 1) * 64], attention))
            if s == 0 and p == 1:
                plane_step(p - 1)
        mixs[:, p * 128 : (p + 1) * 128] = mixed.astype(BF16)
        act_part = jnp.concatenate([(dq * 0.125).astype(BF16), jnp.concatenate(dk_t + dv_t, axis=0).astype(BF16).T], axis=1)
        s1[p] = dot(normed_t, act_part).astype(BF16).reshape(2, 256, CHUNK)
        send(s1.at[p, 1 - core], r1.at[p], sem_s1.at[p], sem_r1.at[p], twin)
        w_part = jnp.concatenate([w_qkv[:, j * D + p * 128 : j * D + (p + 1) * 128] for j in range(3)], axis=1)
        grad_normed = grad_normed + dot_nt(act_part, w_part)
        if p == PAIRS - 2:
            table_step(range(HEADS - 2))

    table_step(range(HEADS - 2, HEADS))
    grad_normed = grad_normed.astype(BF16).astype(F32)
    gain_part = jnp.sum(grad_normed * xhat, axis=0, keepdims=True)
    for j in range(4):
        ex[12, j : j + 1, :] = gain_part[:, j * 128 : (j + 1) * 128]
    def share_plane(i, carry):
        d = far_first(i)
        other, to = plane_at(d)
        send(ex.at[other], rx2.at[d - 1], sem_xs.at[0], sem_xr.at[0], to)
        return carry

    lax.fori_loop(1, N_PLANE, share_plane, 0)
    plane_step(1)
    plane_step(PAIRS - 2)
    plane_step(PAIRS - 1)

    grad_hat = grad_normed * gain[...]
    shift = jnp.mean(grad_hat, axis=-1, keepdims=True)
    slope = jnp.mean(grad_hat * xhat, axis=-1, keepdims=True)
    dx = cot + rstd * (grad_hat - shift - xhat * slope)
    out = x + dot(mixs[...], w_proj[...]).astype(BF16).astype(F32)
    own = []
    for a, (values, ref) in enumerate(((out, result), (dx, grad_in))):
        for l in range(LEVELS):
            for j in range(4):
                line_up[pl.ds(2 * j + l, 72, stride=8), :] = values[l * 72 : (l + 1) * 72, j * 128 : (j + 1) * 128]
        fin[a] = line_up[...].reshape(WLAT, WLON, 8, 128).astype(BF16)
        for quad in range(3):
            send(window_part(fin.at[a], quad), token_part(ref, quad), sem_bs.at[quad, a], sem_br.at[quad, a], back_to[quad])
        own.append(pltpu.make_async_copy(window_part(fin.at[a], 3), token_part(ref, 3), sem_own.at[a]))
        own[-1].start()

    def z_step(p):
        wait(r2.at[p], sem_r2.at[p])
        total = s2[p, plane].astype(F32)
        for d in range(N_PLANE - 1):
            total = total + r2[p, d].astype(F32)
        for row in range(N_Z):
            s3[p, row] = total[row : row + 1]

        def one(i, carry):
            d = far_first(i)
            other, to = z_at(d)
            send(s3.at[p, other], r3.at[p, d - 1], sem_s3.at[p], sem_r3.at[p], to)
            return carry

        lax.fori_loop(1, N_Z, one, 0)

    pl.semaphore_wait(relay, 2)
    wait(rx2, sem_xr.at[0])
    rx3[z] = ex[plane] + jnp.sum(rx2[...], axis=0)

    def share_z(i, carry):
        send(rx3.at[z], rx3.at[z], sem_xs.at[1], sem_xr.at[1], z_at(far_first(i))[1])
        return carry

    lax.fori_loop(1, N_Z, share_z, 0)
    for p in range(PAIRS):
        z_step(p)

    wait(rx3.at[0:15], sem_xr.at[1])
    wait(rx3.at[0:15], sem_xs.at[1])
    mine = core * N_PLANE + plane
    rx4[mine] = jnp.sum(rx3[...], axis=0)

    def share_back(i, carry):
        d = far_first(i)
        send(rx4.at[mine], rx4.at[mine], sem_xs.at[2], sem_xr.at[2], plane_at(d)[1])
        send(rx4.at[mine], rx4.at[mine], sem_xs.at[2], sem_xr.at[2], plane_at(d, 1 - core)[1])
        return carry

    lax.fori_loop(1, N_PLANE, share_back, 0)
    send(rx4.at[mine], rx4.at[mine], sem_xs.at[2], sem_xr.at[2], twin)

    for p in range(PAIRS):
        wait(r3.at[p], sem_r3.at[p])
        line = s3[p, z] + jnp.sum(r3[p], axis=0)
        for j in range(3):
            grad_qkv[:, j * D + p * 128 : j * D + (p + 1) * 128] = line[:, j * 128 : (j + 1) * 128]
    own.append(pltpu.make_async_copy(grad_qkv, qkv_hbm, sem_out.at[2]))
    own[-1].start()
    wait(rx4.at[0:31], sem_xr.at[2])
    sums = rx4[0:N_PLANE] + rx4[N_PLANE : 2 * N_PLANE]
    for j in range(4):
        grad_gain[:, j * 128 : (j + 1) * 128] = sums[12, j : j + 1, :]
    for j in range(6):
        width = min(128, RELN - j * 128)
        for half in range(2):
            grad_bias[half * 4 : half * 4 + 4, j * 128 : j * 128 + width] = sums[2 * j + half, :, 0:width]
    for i, (src, dst) in enumerate(((grad_gain, dgain_hbm), (grad_bias, dbias_hbm))):
        own.append(pltpu.make_async_copy(src, dst, sem_out.at[i]))
        own[-1].start()

    for copy in own:
        copy.wait()
    for quad in range(3):
        for a, ref in enumerate((result, grad_in)):
            wait(token_part(ref, quad), sem_br.at[quad, a])
            wait(token_part(ref, quad), sem_bs.at[quad, a])
            wait(window_part(win.at[a], quad), sem_hs.at[quad, a])
        wait(khs.at[quad], sem_hs.at[quad, 2])
    for p in range(PAIRS):
        wait(r1.at[p], sem_s1.at[p])
        wait(r2.at[p], sem_s2.at[p])
        wait(r3.at[p], sem_s3.at[p])
    wait(rx2, sem_xs.at[0])
    wait(rx4.at[0:31], sem_xs.at[2])


def finish(*refs):
    ins, outs, held, sem_in, sem_out = refs[:5], refs[5:10], refs[10:15], refs[15], refs[16]
    arrivals = [pltpu.make_async_copy(src, mid, sem_in.at[i]) for i, (src, mid) in enumerate(zip(ins, held))]
    leaves = [pltpu.make_async_copy(mid, dst, sem_out.at[i]) for i, (mid, dst) in enumerate(zip(held, outs))]
    for copy in arrivals:
        copy.start()
    for arrival, leave in zip(arrivals, leaves):
        arrival.wait()
        leave.start()
    for copy in leaves:
        copy.wait()


def to_tiles(x):
    return x.transpose(1, 2, 0, 3).reshape(WLAT, WLON, LEVELS, 4, 128).transpose(0, 1, 3, 2, 4).reshape(WLAT, WLON, 8, 128)


def from_tiles(x):
    x = x.reshape(WLAT, WLON, 4, LEVELS, 128).transpose(0, 1, 3, 2, 4).reshape(WLAT, WLON, LEVELS, D)
    return x.transpose(2, 0, 1, 3)


def local(tokens, key_valid, norm_gain, w_qkv, bias_table, w_proj, grad_out):
    hbm = pl.BlockSpec(memory_space=pl.ANY)
    tables = make_tables()
    dma = pltpu.SemaphoreType.DMA
    operands = (
        to_tiles(tokens), key_valid.transpose(1, 0, 2), norm_gain.reshape(1, D), w_qkv, bias_table, w_proj, to_tiles(grad_out),
    ) + tables
    loaded = [operands[i] for i in (1, 2, 3, 4, 5)] + list(tables)
    shapes = (
        jax.ShapeDtypeStruct((WLAT, WLON, 8, 128), BF16),
        jax.ShapeDtypeStruct((WLAT, WLON, 8, 128), BF16),
        jax.ShapeDtypeStruct((1, 3 * D), F32),
        jax.ShapeDtypeStruct((1, D), F32),
        jax.ShapeDtypeStruct((HEADS, RELN), F32),
    )
    parts = pl.pallas_call(
        kernel,
        out_shape=shapes,
        in_specs=[hbm] * len(operands),
        out_specs=[hbm] * 5,
        scratch_shapes=[pltpu.VMEM(v.shape, v.dtype) for v in list(shapes[2:]) + loaded] + [
            pltpu.VMEM((2, WLAT, WLON, 8, 128), BF16),
            pltpu.VMEM((2, WLAT, WLON, 8, 128), BF16),
            pltpu.VMEM((8 * 72, 128), F32),
            pltpu.VMEM((16, 128), F32),
            pltpu.VMEM((HEADS, RELP), F32),
            pltpu.VMEM((3, 1, 256), F32),
            pltpu.VMEM((4, 1, 256), F32),
            pltpu.VMEM((HEADS, WIN, WIN), F32),
            pltpu.VMEM((WIN, WIN), F32),
            pltpu.VMEM((HEADS, WIN, WIN), F32),
            pltpu.VMEM((12, WIN, 128), BF16),
            pltpu.VMEM((4, WIN, 128), BF16),
            pltpu.VMEM((WIN, D), BF16),
            pltpu.VMEM((PAIRS, 2, 256, CHUNK), BF16),
            pltpu.VMEM((PAIRS, 256, CHUNK), BF16),
            pltpu.VMEM((PAIRS, N_PLANE, N_Z, CHUNK), BF16),
            pltpu.VMEM((PAIRS, N_PLANE - 1, N_Z, CHUNK), BF16),
            pltpu.VMEM((PAIRS, N_Z, 1, CHUNK), F32),
            pltpu.VMEM((PAIRS, N_Z - 1, 1, CHUNK), F32),
            pltpu.VMEM((16, 4, 128), F32),
            pltpu.VMEM((15, 4, 128), F32),
            pltpu.VMEM((16, 4, 128), F32),
            pltpu.VMEM((32, 4, 128), F32),
            dma((len(loaded),)), dma((2,)), dma((3,)), dma((3, 3)), dma((3, 3)), dma((3, 2)), dma((3, 2)),
            dma((PAIRS,)), dma((PAIRS,)), dma((PAIRS,)), dma((PAIRS,)),
            dma((PAIRS,)), dma((PAIRS,)), dma((3,)), dma((3,)), pltpu.SemaphoreType.REGULAR,
        ],
        compiler_params=pltpu.CompilerParams(
            collective_id=0, has_side_effects=True, vmem_limit_bytes=VMEM_LIMIT
        ),
        name="window_block",
    )(*operands)
    result, grad_in, grad_qkv, grad_gain, grad_bias = pl.pallas_call(
        finish,
        out_shape=shapes,
        in_specs=[hbm] * 5,
        out_specs=[hbm] * 5,
        scratch_shapes=[pltpu.VMEM(v.shape, v.dtype) for v in shapes] + [dma((5,)), dma((5,))],
        compiler_params=pltpu.CompilerParams(vmem_limit_bytes=VMEM_LIMIT),
        name="finish",
    )(*parts)
    return from_tiles(result), from_tiles(grad_in), grad_qkv, grad_gain.reshape(D), grad_bias


def solution(mesh):
    placed = (
        P(None, "lat", "lon", None),
        P(None, "lat", "lon"),
        P(),
        P(),
        P(),
        P(),
        P(None, "lat", "lon", None),
    )
    return jax.shard_map(
        local,
        mesh=mesh,
        in_specs=placed,
        out_specs=(
            P(None, "lat", "lon", None),
            P(None, "lat", "lon", None),
            P(("lon", "lat"), None),
            P(),
            P(),
        ),
        check_vma=False,
    )
```

```python
import jax
import jax.numpy as jnp
import numpy as np
from jax import lax
from jax.experimental import pallas as pl
from jax.experimental.pallas import tpu as pltpu
from jax.sharding import PartitionSpec as P

MESH = pl.DeviceIdType.MESH
F32 = jnp.float32
BF16 = jnp.bfloat16

LEVELS, WLAT, WLON = 2, 6, 12
WIN = LEVELS * WLAT * WLON
D = 512
HEADS = 8
PAIRS = HEADS // 2
RELN = 759
RELP = 768
N_LON, N_LAT = 64, 8
N_Z = 16
N_PLANE = 16
CHUNK = 3 * 128
VMEM_LIMIT = 60 * 1024 * 1024


def offset_of(t):
    level, row, col = t // 72, t // 12 % 6, t % 12
    return 253 * level + 23 * row + col


def make_tables():
    key_col = np.zeros((128, 256), np.float32)
    key_row = np.zeros((4, 16, 256), np.float32)
    for l in range(LEVELS):
        for r in range(WLAT):
            for c in range(WLON):
                t = l * 72 + ((r + 3) % 6) * 12 + (c + 6) % 12
                key_col[c, t] = 1
                key_row[(r // 3) * 2 + c // 6, r * 2 + l, t] = 1
    perm = np.zeros((D, D), np.float32)
    for core in range(2):
        for xh in range(2):
            for lat in range(8):
                for z in range(16):
                    perm[core * 256 + (xh * 8 + lat) * 16 + z, xh * 256 + z * 16 + core * 8 + lat] = 1
    pick = np.zeros((6, WIN, RELP), np.float32)
    for g in range(6):
        for k in range(WIN):
            pick[g, k, (379 + 253 * (g // 3) + 46 * (g % 3) - offset_of(k)) % RELP] = 1
    step = np.arange(24)
    step = np.tile(23 * (step // 12) + step % 12, HEADS)
    skew = np.broadcast_to(step[:, None], (192, 128)).astype(np.int32)
    half = np.arange(WIN) // 12 % 6 >= 3
    masks = np.stack([half[:, None] != half[None, :], np.eye(WIN, dtype=bool)]).astype(np.float32)
    as_bf16 = lambda v: jnp.asarray(v, BF16)
    return (
        as_bf16(key_col),
        jnp.asarray(key_row),
        jnp.asarray(skew),
        as_bf16(pick),
        jnp.asarray(masks),
        as_bf16(perm),
    )


def dot(a, b):
    return lax.dot_general(a, b, (((1,), (0,)), ((), ())), preferred_element_type=F32)


def dot_nt(a, b):
    return lax.dot_general(a, b, (((1,), (1,)), ((), ())), preferred_element_type=F32)


def dot_tn(a, b):
    return lax.dot_general(a, b, (((0,), (0,)), ((), ())), preferred_element_type=F32)


def skewed(rows, skew, left):
    for bit in (1, 2, 4, 8, 16, 32):
        moved = pltpu.roll(rows, RELP - bit if left else bit, 1)
        rows = jnp.where((skew & bit) != 0, moved, rows)
    return rows


def window_part(ref, quad):
    return ref.at[pl.ds(3 - 3 * (quad // 2), 3), pl.ds(6 - 6 * (quad % 2), 6)]


def token_part(ref, quad):
    return ref.at[pl.ds(3 * (quad // 2), 3), pl.ds(6 * (quad % 2), 6)]


def kernel(
    tok_hbm, kv_hbm, gain_hbm, w_qkv_hbm, table_hbm, w_proj_hbm, gout_hbm,
    key_col_hbm, key_row_hbm, skew_hbm, pick_hbm, masks_hbm, perm_hbm,
    result, grad_in, qkv_hbm, dgain_hbm, dbias_hbm,
    grad_qkv, grad_gain, grad_bias, kv, gain, w_qkv, table, w_proj, key_col, key_row, skew_ref, pick, masks, perm,
    win, fin, line_up, kvs, tabs, khs, khr, bias, allowed, dscore,
    qkvs, gms, mixs, s1, r1, s2, r2, s3, r3, ex, rx2, rx3, rx4,
    sem_in, sem_own, sem_out, sem_hs, sem_hr, sem_bs, sem_br, sem_s1, sem_r1, sem_s2, sem_r2, sem_s3, sem_r3, sem_xs, sem_xr, relay,
):
    lon, lat = lax.axis_index("lon"), lax.axis_index("lat")
    xh, zc = lax.div(lon, 32), lax.rem(lon, 32)
    z, core = lax.div(zc, 2), lax.rem(zc, 2)
    plane = xh * 8 + lat
    x_at, y_at = lax.div(plane, 4), lax.rem(plane, 4)
    west, east = lax.rem(lon + N_LON - 1, N_LON), lax.rem(lon + 1, N_LON)
    north, south = lax.rem(lat + N_LAT - 1, N_LAT), lax.rem(lat + 1, N_LAT)
    twin = {"lon": lon + 1 - 2 * core, "lat": lat}
    halo_to = ({"lon": west, "lat": north}, {"lon": lon, "lat": north}, {"lon": west, "lat": lat})
    back_to = ({"lon": east, "lat": south}, {"lon": lon, "lat": south}, {"lon": east, "lat": lat})

    def plane_at(d, on=core):
        slow, fast = lax.div(d, 4), lax.rem(d, 4)
        x_to = lax.rem(x_at + slow + core * (fast - slow), 4)
        y_to = lax.rem(y_at + fast + core * (slow - fast), 4)
        other = x_to * 4 + y_to
        return other, {"lon": lax.div(x_to, 2) * 32 + z * 2 + on, "lat": lax.rem(x_to, 2) * 4 + y_to}

    def z_at(d):
        other = lax.rem(z + d, N_Z)
        return other, {"lon": xh * 32 + other * 2 + core, "lat": lat}

    def far_first(i):
        return 8 + lax.div(i, 2) * (1 - 2 * lax.rem(i, 2))

    def send(src, dst, send_sem, recv_sem, to):
        pltpu.make_async_remote_copy(
            src_ref=src, dst_ref=dst, send_sem=send_sem, recv_sem=recv_sem,
            device_id=to, device_id_type=MESH,
        ).start()

    def wait(ref, sem):
        pltpu.make_async_copy(ref, ref, sem).wait()

    barrier = pltpu.get_barrier_semaphore()

    def greet(to):
        pl.semaphore_signal(barrier, inc=1, device_id=to, device_id_type=MESH)

    def greet_both(i, carry):
        greet(plane_at(i)[1])
        greet(plane_at(i, 1 - core)[1])
        return carry

    for to in halo_to + back_to + (twin,):
        greet(to)
    loads = []
    for i, (src, dst) in enumerate((
        (kv_hbm, kv), (key_col_hbm, key_col), (key_row_hbm, key_row), (table_hbm, table), (skew_hbm, skew_ref),
        (pick_hbm, pick), (masks_hbm, masks), (gain_hbm, gain), (w_qkv_hbm, w_qkv), (w_proj_hbm, w_proj), (perm_hbm, perm),
    )):
        loads.append(pltpu.make_async_copy(src, dst, sem_in.at[i]))
    in_kv, in_key_col, in_key_row, in_table, in_skew, in_pick, in_masks, in_gain, in_w_qkv, in_w_proj, in_perm = loads
    for load in loads[:3]:
        load.start()
    for d in (4, 12, 3, 13, 2, 14, 1, 15):
        greet(z_at(d)[1])
    lax.fori_loop(1, N_PLANE, greet_both, 0)

    for load in loads[3:]:
        load.start()
    own = [
        pltpu.make_async_copy(token_part(ref, 3), window_part(win.at[a], 3), sem_own.at[a])
        for a, ref in enumerate((tok_hbm, gout_hbm))
    ]
    for copy in own:
        copy.start()

    pl.semaphore_wait(barrier, 45)
    for quad in range(3):
        for a, ref in enumerate((tok_hbm, gout_hbm)):
            send(token_part(ref, quad), window_part(win.at[a], quad), sem_hs.at[quad, a], sem_hr.at[quad, a], halo_to[quad])
    for d in (4, 12):
        pl.semaphore_signal(relay, inc=1, device_id=z_at(d)[1], device_id_type=MESH)

    for ready in (in_kv, in_key_col, in_key_row):
        ready.wait()
    kvs[...] = jnp.zeros_like(kvs)
    for r in range(WLAT):
        kvs[r * 2 : r * 2 + 2, 0:WLON] = kv[r].astype(F32)
    keys = dot(kvs[...].astype(BF16), key_col[...])
    for quad in range(4):
        key_line = jnp.sum(keys * key_row[quad], axis=0, keepdims=True)
        if quad == 3:
            khr[3] = key_line
        else:
            khs[quad] = key_line
            send(khs.at[quad], khr.at[quad], sem_hs.at[quad, 2], sem_hr.at[quad, 2], halo_to[quad])

    for ready in (in_table, in_skew, in_pick):
        ready.wait()
    tabs[...] = jnp.zeros_like(tabs)
    tabs[:, 0:RELN] = table[...]
    skew = jnp.broadcast_to(skew_ref[:, 0:1], (192, RELP))
    rows = jnp.concatenate(
        [jnp.broadcast_to(tabs[h : h + 1, :], (24, RELP)) for h in range(HEADS)], axis=0
    )
    rows = skewed(rows, skew, True)
    high = rows.astype(BF16)
    low = (rows - high.astype(F32)).astype(BF16)
    both = jnp.concatenate([high, low], axis=0)
    for g in range(6):
        part = dot_nt(both, pick[g])
        part = part[:192] + part[192:]
        for h in range(HEADS):
            bias[h, g * 24 : (g + 1) * 24, :] = part[h * 24 : (h + 1) * 24]

    for copy in own:
        copy.wait()
    for quad in range(3):
        for a in range(2):
            wait(window_part(win.at[a], quad), sem_hr.at[quad, a])
        wait(khr.at[quad], sem_hr.at[quad, 2])
    for ready in (in_masks, in_gain, in_w_qkv, in_w_proj, in_perm):
        ready.wait()

    def gather(a):
        line_up[...] = win[a].astype(F32).reshape(8 * 72, 128)
        levels = []
        for l in range(LEVELS):
            parts = [line_up[pl.ds(2 * j + l, 72, stride=8), :] for j in range(4)]
            levels.append(jnp.concatenate(parts, axis=1))
        return jnp.concatenate(levels, axis=0)

    x = gather(0)
    cot = gather(1)
    key_ok = (khr[0] + khr[1] + khr[2] + khr[3])[:, 0:WIN]
    edge = (lat == N_LAT - 1).astype(F32)
    allowed[...] = (1.0 - edge * masks[0]) * jnp.maximum(key_ok, masks[1])

    centred = x - jnp.mean(x, axis=-1, keepdims=True)
    spread = jnp.mean(centred * centred, axis=-1, keepdims=True)
    rstd = lax.rsqrt(spread + 1e-5)
    xhat = centred * rstd
    normed = (xhat * gain[...]).astype(BF16)
    act = dot(normed, w_qkv[...]).astype(BF16)
    grad_mixed = dot_nt(cot.astype(BF16), w_proj[...]).astype(BF16)
    for j in range(12):
        qkvs[j] = act[:, j * 128 : (j + 1) * 128]
    for j in range(4):
        gms[j] = grad_mixed[:, j * 128 : (j + 1) * 128]
    normed_t = dot_nt(perm[...], normed).astype(BF16)
    first = lax.broadcasted_iota(jnp.int32, (WIN, 128), 1) < 64

    def plane_step(p):
        wait(r1.at[p], sem_r1.at[p])
        s2[p] = (s1[p, core].astype(F32) + r1[p].astype(F32)).astype(BF16).reshape(N_PLANE, N_Z, CHUNK)

        def one(i, carry):
            d = far_first(i)
            other, to = plane_at(d)
            send(s2.at[p, other], r2.at[p, d - 1], sem_s2.at[p], sem_r2.at[p], to)
            return carry

        lax.fori_loop(1, N_PLANE, one, 0)

    def table_step(heads):
        part = jnp.zeros((24 * len(heads), RELP), F32)
        for g in range(6):
            group = jnp.concatenate([dscore[h, g * 24 : (g + 1) * 24, :] for h in heads], axis=0)
            part = part + dot(group.astype(BF16), pick[g])
        part = skewed(part, skew[: 24 * len(heads)], False)
        for s, h in enumerate(heads):
            line = jnp.sum(part[s * 24 : (s + 1) * 24], axis=0, keepdims=True)
            for j in range(6):
                ex[2 * j + h // 4, h % 4 : h % 4 + 1, :] = line[:, j * 128 : (j + 1) * 128]

    ex[...] = jnp.zeros_like(ex)
    grad_normed = jnp.zeros((WIN, D), F32)
    for p in range(PAIRS):
        q2, k2, v2, gm2 = qkvs[p], qkvs[4 + p], qkvs[8 + p], gms[p]
        zero = jnp.zeros_like(q2)
        mixed = dq = jnp.zeros((WIN, 128), F32)
        q_t, gm_t = (q2 * jnp.asarray(0.125, BF16)).T, gm2.T
        dk_t, dv_t = [], []
        for s in range(2):
            h = 2 * p + s
            mine = first if s == 0 else jnp.logical_not(first)
            qm = jnp.where(mine, q2, zero) * jnp.asarray(0.125, BF16)
            km = jnp.where(mine, k2, zero)
            vm = jnp.where(mine, v2, zero)
            gm = jnp.where(mine, gm2, zero)
            weights = jnp.exp(dot_nt(qm, k2) + bias[h]) * allowed[...]
            probs = weights * (1.0 / jnp.sum(weights, axis=-1, keepdims=True))
            attention = probs.astype(BF16)
            mixed = mixed + dot(attention, vm)
            grad_att = dot_nt(gm, v2).astype(BF16).astype(F32)
            pull = probs * grad_att
            grad_scores = pull - probs * jnp.sum(pull, axis=-1, keepdims=True)
            dscore[h] = grad_scores
            short = grad_scores.astype(BF16)
            dq = dq + dot(short, km)
            dk_t.append(dot(q_t[s * 64 : (s + 1) * 64], short))
            dv_t.append(dot(gm_t[s * 64 : (s + 1) * 64], attention))
            if s == 0 and p == 1:
                plane_step(p - 1)
        mixs[:, p * 128 : (p + 1) * 128] = mixed.astype(BF16)
        act_part = jnp.concatenate([(dq * 0.125).astype(BF16), jnp.concatenate(dk_t + dv_t, axis=0).astype(BF16).T], axis=1)
        s1[p] = dot(normed_t, act_part).astype(BF16).reshape(2, 256, CHUNK)
        send(s1.at[p, 1 - core], r1.at[p], sem_s1.at[p], sem_r1.at[p], twin)
        w_part = jnp.concatenate([w_qkv[:, j * D + p * 128 : j * D + (p + 1) * 128] for j in range(3)], axis=1)
        grad_normed = grad_normed + dot_nt(act_part, w_part)
        if p == PAIRS - 2:
            table_step(range(HEADS - 2))

    table_step(range(HEADS - 2, HEADS))
    grad_normed = grad_normed.astype(BF16).astype(F32)
    gain_part = jnp.sum(grad_normed * xhat, axis=0, keepdims=True)
    for j in range(4):
        ex[12, j : j + 1, :] = gain_part[:, j * 128 : (j + 1) * 128]
    def share_plane(i, carry):
        d = far_first(i)
        other, to = plane_at(d)
        send(ex.at[other], rx2.at[d - 1], sem_xs.at[0], sem_xr.at[0], to)
        return carry

    lax.fori_loop(1, N_PLANE, share_plane, 0)
    plane_step(1)
    plane_step(PAIRS - 2)
    plane_step(PAIRS - 1)

    grad_hat = grad_normed * gain[...]
    shift = jnp.mean(grad_hat, axis=-1, keepdims=True)
    slope = jnp.mean(grad_hat * xhat, axis=-1, keepdims=True)
    dx = cot + rstd * (grad_hat - shift - xhat * slope)
    out = x + dot(mixs[...], w_proj[...]).astype(BF16).astype(F32)
    own = []
    for a, (values, ref) in enumerate(((out, result), (dx, grad_in))):
        for l in range(LEVELS):
            for j in range(4):
                line_up[pl.ds(2 * j + l, 72, stride=8), :] = values[l * 72 : (l + 1) * 72, j * 128 : (j + 1) * 128]
        fin[a] = line_up[...].reshape(WLAT, WLON, 8, 128).astype(BF16)
        for quad in range(3):
            send(window_part(fin.at[a], quad), token_part(ref, quad), sem_bs.at[quad, a], sem_br.at[quad, a], back_to[quad])
        own.append(pltpu.make_async_copy(window_part(fin.at[a], 3), token_part(ref, 3), sem_own.at[a]))
        own[-1].start()

    def z_step(p):
        wait(r2.at[p], sem_r2.at[p])
        total = s2[p, plane].astype(F32)
        for d in range(N_PLANE - 1):
            total = total + r2[p, d].astype(F32)
        for row in range(N_Z):
            s3[p, row] = total[row : row + 1]

        def one(i, carry):
            d = far_first(i)
            other, to = z_at(d)
            send(s3.at[p, other], r3.at[p, d - 1], sem_s3.at[p], sem_r3.at[p], to)
            return carry

        lax.fori_loop(1, N_Z, one, 0)

    pl.semaphore_wait(relay, 2)
    wait(rx2, sem_xr.at[0])
    rx3[z] = ex[plane] + jnp.sum(rx2[...], axis=0)

    def share_z(i, carry):
        send(rx3.at[z], rx3.at[z], sem_xs.at[1], sem_xr.at[1], z_at(far_first(i))[1])
        return carry

    lax.fori_loop(1, N_Z, share_z, 0)
    for p in range(PAIRS):
        z_step(p)

    wait(rx3.at[0:15], sem_xr.at[1])
    wait(rx3.at[0:15], sem_xs.at[1])
    mine = core * N_PLANE + plane
    rx4[mine] = jnp.sum(rx3[...], axis=0)

    def share_back(i, carry):
        d = far_first(i)
        send(rx4.at[mine], rx4.at[mine], sem_xs.at[2], sem_xr.at[2], plane_at(d)[1])
        send(rx4.at[mine], rx4.at[mine], sem_xs.at[2], sem_xr.at[2], plane_at(d, 1 - core)[1])
        return carry

    lax.fori_loop(1, N_PLANE, share_back, 0)
    send(rx4.at[mine], rx4.at[mine], sem_xs.at[2], sem_xr.at[2], twin)

    for p in range(PAIRS):
        wait(r3.at[p], sem_r3.at[p])
        line = s3[p, z] + jnp.sum(r3[p], axis=0)
        for j in range(3):
            grad_qkv[:, j * D + p * 128 : j * D + (p + 1) * 128] = line[:, j * 128 : (j + 1) * 128]
    own.append(pltpu.make_async_copy(grad_qkv, qkv_hbm, sem_out.at[2]))
    own[-1].start()
    wait(rx4.at[0:31], sem_xr.at[2])
    sums = rx4[0:N_PLANE] + rx4[N_PLANE : 2 * N_PLANE]
    for j in range(4):
        grad_gain[:, j * 128 : (j + 1) * 128] = sums[12, j : j + 1, :]
    for j in range(6):
        width = min(128, RELN - j * 128)
        for half in range(2):
            grad_bias[half * 4 : half * 4 + 4, j * 128 : j * 128 + width] = sums[2 * j + half, :, 0:width]
    for i, (src, dst) in enumerate(((grad_gain, dgain_hbm), (grad_bias, dbias_hbm))):
        own.append(pltpu.make_async_copy(src, dst, sem_out.at[i]))
        own[-1].start()

    for copy in own:
        copy.wait()
    for quad in range(3):
        for a, ref in enumerate((result, grad_in)):
            wait(token_part(ref, quad), sem_br.at[quad, a])
            wait(token_part(ref, quad), sem_bs.at[quad, a])
            wait(window_part(win.at[a], quad), sem_hs.at[quad, a])
        wait(khs.at[quad], sem_hs.at[quad, 2])
    for p in range(PAIRS):
        wait(r1.at[p], sem_s1.at[p])
        wait(r2.at[p], sem_s2.at[p])
        wait(r3.at[p], sem_s3.at[p])
    wait(rx2, sem_xs.at[0])
    wait(rx4.at[0:31], sem_xs.at[2])


def finish(*refs):
    ins, outs, held, sem_in, sem_out = refs[:5], refs[5:10], refs[10:15], refs[15], refs[16]
    arrivals = [pltpu.make_async_copy(src, mid, sem_in.at[i]) for i, (src, mid) in enumerate(zip(ins, held))]
    leaves = [pltpu.make_async_copy(mid, dst, sem_out.at[i]) for i, (mid, dst) in enumerate(zip(held, outs))]
    for copy in arrivals:
        copy.start()
    for arrival, leave in zip(arrivals, leaves):
        arrival.wait()
        leave.start()
    for copy in leaves:
        copy.wait()


def to_tiles(x):
    return x.transpose(1, 2, 0, 3).reshape(WLAT, WLON, LEVELS, 4, 128).transpose(0, 1, 3, 2, 4).reshape(WLAT, WLON, 8, 128)


def from_tiles(x):
    x = x.reshape(WLAT, WLON, 4, LEVELS, 128).transpose(0, 1, 3, 2, 4).reshape(WLAT, WLON, LEVELS, D)
    return x.transpose(2, 0, 1, 3)


def local(tokens, key_valid, norm_gain, w_qkv, bias_table, w_proj, grad_out):
    hbm = pl.BlockSpec(memory_space=pl.ANY)
    tables = make_tables()
    dma = pltpu.SemaphoreType.DMA
    operands = (
        to_tiles(tokens), key_valid.transpose(1, 0, 2), norm_gain.reshape(1, D), w_qkv, bias_table, w_proj, to_tiles(grad_out),
    ) + tables
    loaded = [operands[i] for i in (1, 2, 3, 4, 5)] + list(tables)
    shapes = (
        jax.ShapeDtypeStruct((WLAT, WLON, 8, 128), BF16),
        jax.ShapeDtypeStruct((WLAT, WLON, 8, 128), BF16),
        jax.ShapeDtypeStruct((1, 3 * D), F32),
        jax.ShapeDtypeStruct((1, D), F32),
        jax.ShapeDtypeStruct((HEADS, RELN), F32),
    )
    parts = pl.pallas_call(
        kernel,
        out_shape=shapes,
        in_specs=[hbm] * len(operands),
        out_specs=[hbm] * 5,
        scratch_shapes=[pltpu.VMEM(v.shape, v.dtype) for v in list(shapes[2:]) + loaded] + [
            pltpu.VMEM((2, WLAT, WLON, 8, 128), BF16),
            pltpu.VMEM((2, WLAT, WLON, 8, 128), BF16),
            pltpu.VMEM((8 * 72, 128), F32),
            pltpu.VMEM((16, 128), F32),
            pltpu.VMEM((HEADS, RELP), F32),
            pltpu.VMEM((3, 1, 256), F32),
            pltpu.VMEM((4, 1, 256), F32),
            pltpu.VMEM((HEADS, WIN, WIN), F32),
            pltpu.VMEM((WIN, WIN), F32),
            pltpu.VMEM((HEADS, WIN, WIN), F32),
            pltpu.VMEM((12, WIN, 128), BF16),
            pltpu.VMEM((4, WIN, 128), BF16),
            pltpu.VMEM((WIN, D), BF16),
            pltpu.VMEM((PAIRS, 2, 256, CHUNK), BF16),
            pltpu.VMEM((PAIRS, 256, CHUNK), BF16),
            pltpu.VMEM((PAIRS, N_PLANE, N_Z, CHUNK), BF16),
            pltpu.VMEM((PAIRS, N_PLANE - 1, N_Z, CHUNK), BF16),
            pltpu.VMEM((PAIRS, N_Z, 1, CHUNK), F32),
            pltpu.VMEM((PAIRS, N_Z - 1, 1, CHUNK), F32),
            pltpu.VMEM((16, 4, 128), F32),
            pltpu.VMEM((15, 4, 128), F32),
            pltpu.VMEM((16, 4, 128), F32),
            pltpu.VMEM((32, 4, 128), F32),
            dma((len(loaded),)), dma((2,)), dma((3,)), dma((3, 3)), dma((3, 3)), dma((3, 2)), dma((3, 2)),
            dma((PAIRS,)), dma((PAIRS,)), dma((PAIRS,)), dma((PAIRS,)),
            dma((PAIRS,)), dma((PAIRS,)), dma((3,)), dma((3,)), pltpu.SemaphoreType.REGULAR,
        ],
        compiler_params=pltpu.CompilerParams(
            collective_id=0, has_side_effects=True, vmem_limit_bytes=VMEM_LIMIT
        ),
        name="window_block",
    )(*operands)
    result, grad_in, grad_qkv, grad_gain, grad_bias = pl.pallas_call(
        finish,
        out_shape=shapes,
        in_specs=[hbm] * 5,
        out_specs=[hbm] * 5,
        scratch_shapes=[pltpu.VMEM(v.shape, v.dtype) for v in shapes] + [dma((5,)), dma((5,))],
        compiler_params=pltpu.CompilerParams(vmem_limit_bytes=VMEM_LIMIT),
        name="finish",
    )(*parts)
    return from_tiles(result), from_tiles(grad_in), grad_qkv, grad_gain.reshape(D), grad_bias


def solution(mesh):
    placed = (
        P(None, "lat", "lon", None),
        P(None, "lat", "lon"),
        P(),
        P(),
        P(),
        P(),
        P(None, "lat", "lon", None),
    )
    return jax.shard_map(
        local,
        mesh=mesh,
        in_specs=placed,
        out_specs=(
            P(None, "lat", "lon", None),
            P(None, "lat", "lon", None),
            P(("lon", "lat"), None),
            P(),
            P(),
        ),
        check_vma=False,
    )
```
